256 devices in a mesh: tok: 32 (over y, z), exp: 8 (over x, core).
Axes of the slice: x: 4, y: 4, z: 8, core: 2. Of those that a mesh axis runs over, the one named last changes fastest.
Arguments:
- tokens: bfloat16 [4096, 5120], P('tok', 'exp'), may hold values from -6 to 6
- cotangent: bfloat16 [4096, 5120], P('tok', 'exp'), may hold values from -1.796875 to 1.796875
- routes: int32 [4096, 6], P('tok'), may hold values from 0 to 31, as said below
- gate_values: float32 [4096, 6], P('tok'), may hold values from 0.1 to 1
- w_gate: bfloat16 [32, 5120, 1024], P('tok', 'exp'), may hold values from -0.078125 to 0.078125
- w_up: bfloat16 [32, 5120, 1024], P('tok', 'exp'), may hold values from -0.078125 to 0.078125
- w_down: bfloat16 [32, 1024, 5120], P('tok', None, 'exp'), may hold values from -0.1875 to 0.1875
Outputs:
- token_grad: bfloat16 [4096, 5120], P('tok', 'exp')
- gate_grad: bfloat16 [32, 5120, 1024], P('tok', 'exp')
- up_grad: bfloat16 [32, 5120, 1024], P('tok', 'exp')
- down_grad: bfloat16 [32, 1024, 5120], P('tok', None, 'exp')
The draws below stay inside these ranges and needn't reach their ends.
Inputs may be any that keep to these rules, and one draw needn't show every extreme that they name: `routes`: each row names 6 different experts, all within at most 3 of the 8 groups of 4 consecutive expert numbers. Among the 128 rows of one index of tok no expert is named by more than 40 rows, and in every such block some expert is named by exactly 40 rows.
All inputs are finite; a program needn't handle non-finite values.
Results may differ from the reference program's by a relative error of at most 0.033.
Values may be sent and summed in bfloat16 or wider, within the bound.
A program may use at most 128 MiB of HBM per device.

```python
import jax
import jax.numpy as jnp
from jax import lax

D = 5120
FF = 1024
TOPK = 6
EGROUP = 4
TOK_DEV = 128
EXPERTS = 32
GROUPS = 8
CAP = 40
TOKENS = 4096
N_EXP = 8


def draw_routes(key, part):
    key = jax.random.fold_in(key, 11)
    blocks = TOKENS // TOK_DEV
    key_noise, key_favour, key_hot = jax.random.split(key, 3)
    noise = jax.random.randint(key_noise, (blocks, TOK_DEV, EXPERTS), 0, 1024).astype(jnp.int32)
    favour = jax.random.randint(key_favour, (blocks, EXPERTS), 0, 4).astype(jnp.int32)
    hottest = jax.random.randint(key_hot, (blocks,), 0, EXPERTS).astype(jnp.int32)
    expert_ids = jnp.arange(EXPERTS, dtype=jnp.int32)
    group_ids = jnp.arange(GROUPS, dtype=jnp.int32)
    group_count = min(3, GROUPS)

    def one_block(noise_block, favour_row, hot_expert):
        hot_flag = (expert_ids == hot_expert).astype(jnp.int32)

        def step(loads, noise_row):
            usable = loads < CAP
            base_score = hot_flag * 2 ** 26 + favour_row * 2 ** 20 + noise_row * EXPERTS + expert_ids
            expert_score = jnp.where(usable, base_score, -1 - expert_ids)
            usable_count = jnp.sum(usable.astype(jnp.int32).reshape(GROUPS, EGROUP), axis=1)
            hot_usable = (hot_flag * usable.astype(jnp.int32)).reshape(GROUPS, EGROUP)
            hot_group = jnp.max(hot_usable, axis=1)
            group_noise = noise_row.reshape(GROUPS, EGROUP)[:, 0]
            group_score = hot_group * 2 ** 28 + usable_count * 2 ** 24 + group_noise * GROUPS + group_ids
            picked_groups = lax.top_k(group_score, group_count)[1]
            allowed = jnp.any(picked_groups[:, None] == group_ids[None, :], axis=0)
            allowed_expert = jnp.repeat(allowed, EGROUP)
            final_score = jnp.where(allowed_expert, expert_score, -2 ** 30 - expert_ids)
            picks = lax.top_k(final_score, TOPK)[1].astype(jnp.int32)
            added = jnp.sum((picks[:, None] == expert_ids[None, :]).astype(jnp.int32), axis=0)
            return (loads + added, picks)
        start = jnp.zeros((EXPERTS,), dtype=jnp.int32)
        finish, picked = lax.scan(step, start, noise_block)
        return picked
    picked_all = jax.vmap(one_block)(noise, favour, hottest)
    return picked_all.reshape(TOKENS, TOPK).astype(jnp.int32)


def steps_of(key, shape, cuts, smallest, top_value):
    gain, own = 1.0, jax.random.fold_in(key, 6)
    for axis_at, shards_of in cuts:
        steps = jnp.exp(jax.random.uniform(jax.random.fold_in(own, axis_at), (shards_of,), jnp.float32, smallest / len(cuts), top_value / len(cuts)))
        gain = gain * jnp.repeat(steps, shape[axis_at] // shards_of).reshape([-1 if axis == axis_at else 1 for axis in range(len(shape))])
    return gain


def normal_values(rng, extent, spread, most, cuts=(), kind=jnp.bfloat16):
    array = jax.random.normal(rng, extent, jnp.float32) * spread
    if len(cuts) > 0:
        array = steps_of(rng, extent, cuts, -0.22, 0.18) * array
    return jnp.clip(array, min=-most, max=most).astype(kind)


def setup_inputs(seed: int = 0) -> dict:
    streams_of = jax.random.split(jax.random.key(seed), 8)
    tokens = normal_values(streams_of[0], (TOKENS, D), 1.0, 6.0, ((0, 32), (1, 8)))
    cotangent = normal_values(streams_of[1], (TOKENS, D), 0.3, 1.796875, ((0, 32), (1, 8)))
    routes = draw_routes(jax.random.fold_in(streams_of[7], 71), 0)
    gate_values = jnp.clip(0.1 + 0.9 * jax.random.uniform(streams_of[3], (TOKENS, TOPK), jnp.float32) ** steps_of(streams_of[3], (TOKENS, TOPK), ((0, 32),), -0.2, 0.2), 0.1, 1.0)
    w_gate = normal_values(streams_of[4], (EXPERTS, D, FF), D ** -0.5, 0.078125, ((0, 32), (1, 8)))
    w_up = normal_values(streams_of[5], (EXPERTS, D, FF), D ** -0.5, 0.078125, ((0, 32), (1, 8)))
    w_down = normal_values(streams_of[6], (EXPERTS, FF, D), FF ** -0.5, 0.1875, ((0, 32), (2, 8)))
    return dict(tokens=tokens, cotangent=cotangent, routes=routes, gate_values=gate_values, w_gate=w_gate, w_up=w_up, w_down=w_down)


def slot_table(routes, gate_values):
    blocks = TOKENS // TOK_DEV
    flat_routes = routes.reshape(blocks, TOK_DEV * TOPK)
    onehot = (flat_routes[:, :, None] == jnp.arange(EXPERTS, dtype=jnp.int32)[None, None, :]).astype(jnp.int32)
    ranks = jnp.sum((jnp.cumsum(onehot, axis=1) - 1) * onehot, axis=2)
    block_ids = jnp.arange(blocks, dtype=jnp.int32)[:, None]
    slot_ids = (block_ids * CAP + ranks).astype(jnp.int32)
    token_ids = (block_ids * TOK_DEV + jnp.arange(TOK_DEV * TOPK, dtype=jnp.int32)[None, :] // TOPK).astype(jnp.int32)
    table = jnp.full((EXPERTS, blocks * CAP), TOKENS, dtype=jnp.int32)
    table = table.at[flat_routes.reshape(-1), slot_ids.reshape(-1)].set(token_ids.reshape(-1))
    gate_table = jnp.zeros((EXPERTS, blocks * CAP), dtype=jnp.float32)
    gate_table = gate_table.at[flat_routes.reshape(-1), slot_ids.reshape(-1)].set(gate_values.reshape(-1))
    return table, gate_table


def block_sum(parts):
    rounded = lax.optimization_barrier(parts.astype(jnp.bfloat16))
    return jnp.sum(rounded.astype(jnp.float32), axis=0)


def reference(tokens, cotangent, routes, gate_values, w_gate, w_up, w_down):
    table, gate_table = slot_table(routes, gate_values)
    width_block = D // N_EXP
    zero_row = jnp.zeros((1, D), dtype=jnp.bfloat16)
    tokens_pad = jnp.concatenate([tokens, zero_row], axis=0)
    cotangent_pad = jnp.concatenate([cotangent, zero_row], axis=0)

    def per_expert(accum, inputs):
        indices, gate_rows, gate_mat, up_mat, down_mat = inputs
        row_tokens = tokens_pad[indices]
        row_cotan = cotangent_pad[indices]
        scaled = (row_cotan.astype(jnp.float32) * gate_rows[:, None]).astype(jnp.bfloat16)
        split_tokens = row_tokens.reshape(-1, N_EXP, width_block).astype(jnp.float32)
        split_scaled = scaled.reshape(-1, N_EXP, width_block).astype(jnp.float32)
        h_gate = block_sum(jnp.einsum('rnd,ndf->nrf', split_tokens, gate_mat.reshape(N_EXP, width_block, FF).astype(jnp.float32)))
        h_up = block_sum(jnp.einsum('rnd,ndf->nrf', split_tokens, up_mat.reshape(N_EXP, width_block, FF).astype(jnp.float32)))
        d_act = block_sum(jnp.einsum('rnd,fnd->nrf', split_scaled, down_mat.reshape(FF, N_EXP, width_block).astype(jnp.float32)))
        sigmoid_gate = jax.nn.sigmoid(h_gate)
        act = (h_gate * sigmoid_gate * h_up).astype(jnp.bfloat16)
        d_gate = (d_act * h_up * sigmoid_gate * (1.0 + h_gate * (1.0 - sigmoid_gate))).astype(jnp.bfloat16)
        d_up = (d_act * h_gate * sigmoid_gate).astype(jnp.bfloat16)
        down_grad = jnp.dot(act.T, scaled, preferred_element_type=jnp.float32).astype(jnp.bfloat16)
        gate_grad = jnp.dot(row_tokens.T, d_gate, preferred_element_type=jnp.float32).astype(jnp.bfloat16)
        up_grad = jnp.dot(row_tokens.T, d_up, preferred_element_type=jnp.float32).astype(jnp.bfloat16)
        contrib = (jnp.dot(d_gate, gate_mat.T, preferred_element_type=jnp.float32)
                   + jnp.dot(d_up, up_mat.T, preferred_element_type=jnp.float32)).astype(jnp.bfloat16)
        accum = accum.at[indices].add(contrib.astype(jnp.float32))
        return accum, (gate_grad, up_grad, down_grad)

    start = jnp.zeros((TOKENS + 1, D), dtype=jnp.float32)
    accum, grads = lax.scan(per_expert, start, (table, gate_table, w_gate, w_up, w_down))
    token_grad = accum[:TOKENS].astype(jnp.bfloat16)
    return token_grad, grads[0], grads[1], grads[2]
```

```python
import jax
import jax.numpy as jnp
from jax import lax
from jax.experimental import pallas as pl
from jax.experimental.pallas import tpu as pltpu
from jax.sharding import PartitionSpec as P

MESH = pl.DeviceIdType.MESH
F32, BF16 = jnp.float32, jnp.bfloat16

NY, NZ, NX, NC = 4, 8, 4, 2
T = 128
CAP = 40
W = 640
FF = 1024
SH = FF // (NX * NC)
PAIRS = ((0, 1), (3, -3), (4, -2), (2, -1))
PLACE = {off: (c, i) for c, pair in enumerate(PAIRS) for i, off in enumerate(pair)}
YOFF = (0, 1, -1, 2)
YINV = (0, 2, 1, 3)
NCH = len(PAIRS)
NU = 2 * NCH
HALF = 2 * CAP
ROWS = 2 * HALF
DEPTH = 6


def dot(a, b):
    return jnp.dot(a, b, preferred_element_type=F32)


def dot_nt(a, b):
    return lax.dot_general(a, b, (((1,), (1,)), ((), ())), preferred_element_type=F32)


def dot_tn(a, b):
    return lax.dot_general(a, b, (((0,), (0,)), ((), ())), preferred_element_type=F32)


def kernel(
    tok_ref, cot_ref, info_ref, wg_hbm, wu_hbm, wd_hbm,
    tg_ref, gg_hbm, ug_hbm, dg_hbm,
    wg, wu, wd, gg, ug, dg, infob, zx, zd, p2, grow,
    ysx, yss, xr, sr, hp, cr, q, t1, t2, gb, cs, yr, zs, zr, xt,
    info_s, info_r, zx_s, zx_r, zd_s, zd_r, yx_s, yx_r, ys_s, ys_r,
    c1_s, c1_r, x1_s, x1_r, x2_s, x2_r, ag_s, ag_r, cg_s, cg_r,
    yr_s, yr_r, zr_s, zr_r, w_sem, o_sem,
):
    tok = lax.axis_index("tok")
    exp = lax.axis_index("exp")
    y, z = tok // NZ, lax.rem(tok, NZ)
    x, core = exp // NC, lax.rem(exp, NC)

    def at_z(off):
        return (y * NZ + lax.rem(z + off + NZ, NZ), exp)

    def at_y(off):
        return (lax.rem(y + off + NY, NY) * NZ + z, exp)

    def col(off):
        return lax.rem(x + off + NX, NX)

    def at_x(off):
        return (tok, col(off) * NC + core)

    sibling = (tok, x * NC + (1 - core))

    def rc(src, dst, s, r, dev):
        return pltpu.make_async_remote_copy(
            src_ref=src, dst_ref=dst, send_sem=s, recv_sem=r, device_id=dev, device_id_type=MESH
        )

    def info_copy(off):
        return rc(info_ref, infob.at[(NZ - off) % NZ], info_s.at[off], info_r.at[off], at_z(off))

    def z_copy(buf, own, ss, rs, off):
        step = 1 if off > 0 else -1
        before = off - step
        if before == 0:
            src = own
        else:
            src = buf.at[PLACE[before][0], PLACE[before][1]]
        c, i = PLACE[off if off in PLACE else off + NZ]
        k = (off + NZ) % NZ
        return rc(src, buf.at[c, i], ss.at[k], rs.at[k], at_z(-step))

    def zx_copy(off):
        return z_copy(zx, tok_ref, zx_s, zx_r, off)

    def zd_copy(off):
        return z_copy(zd, cot_ref, zd_s, zd_r, off)

    def y_copy(stage, buf, ss, rs, c, k):
        j = YINV[k]
        return rc(stage.at[c, k - 1], buf.at[2 * c + j // 2, j % 2], ss.at[c, k], rs.at[c, j], at_y(YOFF[k]))

    def yx_copy(c, k):
        return y_copy(ysx, xr, yx_s, yx_r, c, k)

    def ys_copy(c, k):
        return y_copy(yss, sr, ys_s, ys_r, c, k)

    def ret_copy(c, k):
        j = YINV[k]
        return rc(
            cs.at[2 * c + k // 2, k % 2], yr.at[2 * c + j // 2, j % 2], yr_s.at[c, k], yr_r.at[c, j], at_y(YOFF[k])
        )

    def c1_copy(u):
        return rc(hp.at[u, 1 - core], cr.at[u], c1_s.at[u], c1_r.at[u], sibling)

    def x1_copy(u, n):
        src, dst, to = (
            (q.at[u, 2, 0], t1.at[u, 0], 1),
            (q.at[u, 2, 1], t1.at[u, 1], -1),
            (q.at[u, 1, 1], t2.at[u, 0, 1], 1),
            (q.at[u, 3, 0], t2.at[u, 1, 0], -1),
        )[n]
        return rc(src, dst, x1_s.at[u, n], x1_r.at[u, n], at_x(to))

    def x2_copy(u, n):
        src, dst, to = ((q.at[u, 1, 0], t2.at[u, 0, 0], 1), (q.at[u, 3, 1], t2.at[u, 1, 1], -1))[n]
        return rc(src, dst, x2_s.at[u, n], x2_r.at[u, n], at_x(to))

    def ag_send(u, n):
        part, to = (
            (gb.at[u, core, x], 1),
            (gb.at[u, core, x], -1),
            (gb.at[u, core, col(-1), 0], 1),
            (gb.at[u, core, col(1), 1], -1),
        )[n]
        return rc(part, part, ag_s.at[u, n], ag_r.at[u, n], at_x(to))

    def ag_wait(u, n):
        part = (
            gb.at[u, core, col(-1)],
            gb.at[u, core, col(1)],
            gb.at[u, core, col(2), 0],
            gb.at[u, core, col(2), 1],
        )[n]
        rc(part, part, ag_s.at[u, n], ag_r.at[u, n], at_x(1)).wait_recv()

    SHARDS = (0, -1, 1, 2)

    def cg_send(u, n):
        part = gb.at[u, core, col(SHARDS[n])]
        return rc(part, part, cg_s.at[u, n], cg_r.at[u, n], sibling)

    def cg_wait(u, n):
        part = gb.at[u, 1 - core, col(SHARDS[n])]
        rc(part, part, cg_s.at[u, n], cg_r.at[u, n], sibling).wait_recv()

    def zr_copy(c, i):
        off = PAIRS[c][i]
        return rc(zs.at[c, i], zr.at[c, i], zr_s.at[c, i], zr_r.at[c, i], at_z(off))

    weights = [
        pltpu.make_async_copy(src, dst, w_sem.at[n])
        for n, (src, dst) in enumerate(((wg_hbm, wg), (wu_hbm, wu), (wd_hbm, wd)))
    ]
    for copy in weights:
        copy.start()
    barrier = pltpu.get_barrier_semaphore()
    partners = [at_z(off) for off in range(1, NZ)] + [at_y(off) for off in (1, -1, 2)]
    partners += [at_x(1), at_x(-1), sibling]
    for dev in partners:
        pl.semaphore_signal(barrier, inc=1, device_id=dev, device_id_type=MESH)
    pl.semaphore_wait(barrier, len(partners))

    for off in range(1, NZ):
        info_copy(off).start()
    for off in (1, -1):
        zx_copy(off).start()
    for off in (1, -1):
        zd_copy(off).start()
    zx[0, 0] = tok_ref[...]
    zd[0, 0] = cot_ref[...]
    infob[0] = info_ref[...]
    for off in range(1, NZ):
        info_copy(off).wait_recv()

    before = (
        lax.broadcasted_iota(jnp.int32, (T, T), 0) < lax.broadcasted_iota(jnp.int32, (T, T), 1)
    ).astype(BF16)
    masks, gates = [], []
    for off in range(NZ):
        block = infob[off]
        ids, vals = block[0:8], block[8:16]
        for k in range(NY):
            expert = (lax.rem(y + YOFF[k] + NY, NY) * NZ + z).astype(F32)
            hit = ids == expert
            masks.append(jnp.sum(jnp.where(hit, 1.0, 0.0), axis=0, keepdims=True))
            gates.append(jnp.sum(jnp.where(hit, vals, 0.0), axis=0, keepdims=True))
    mask_all = jnp.concatenate(masks, axis=0)
    rank_all = dot(mask_all.astype(BF16), before)
    want = lax.broadcasted_iota(jnp.int32, (CAP, T), 0).astype(F32)
    nothing = jnp.zeros((CAP, T), F32)
    for c in range(NCH):
        tables, gcols = [], []
        for k in range(NY):
            for i in range(2):
                n = (PAIRS[c][i] % NZ) * NY + k
                on = (rank_all[n : n + 1] == want) & (mask_all[n : n + 1] > 0.5)
                table = jnp.where(on, 1.0, 0.0)
                gcols.append(jnp.sum(jnp.where(on, gates[n], 0.0), axis=1, keepdims=True))
                tables.append(jnp.concatenate([table, nothing] if i == 0 else [nothing, table], axis=1))
        p2[c] = jnp.concatenate(tables, axis=0).astype(BF16)
        grow[c] = jnp.concatenate(gcols, axis=0)

    def place_x(c):
        rows = dot(p2[c], zx[c].reshape(2 * T, W)).astype(BF16)
        xr[2 * c, 0] = rows[:HALF]
        for k in (1, 2, 3):
            ysx[c, k - 1] = rows[k * HALF : (k + 1) * HALF]
            yx_copy(c, k).start()

    def place_s(c):
        rows = (dot(p2[c], zd[c].reshape(2 * T, W)) * grow[c]).astype(BF16)
        sr[2 * c, 0] = rows[:HALF]
        for k in (1, 2, 3):
            yss[c, k - 1] = rows[k * HALF : (k + 1) * HALF]
            ys_copy(c, k).start()

    def pass_on(copy, d):
        for off in (d, -d):
            copy(off).wait_recv()
        for off in (d + 1, -d - 1):
            if d < 3 or (off > 0) == (copy is zx_copy):
                copy(off).start()

    pass_on(zx_copy, 1)
    place_x(0)
    pass_on(zd_copy, 1)
    place_s(0)
    for copy in weights:
        copy.wait()

    def y_wait(copy, u):
        c, h = u // 2, lax.rem(u, 2)

        @pl.when(h == 0)
        def _():
            copy(c, YINV[1]).wait_recv()

        @pl.when(h == 1)
        def _():
            copy(c, YINV[2]).wait_recv()
            copy(c, YINV[3]).wait_recv()

    def partial(u, a, value):
        value = value.astype(BF16)
        for s in range(NX * NC):
            hp[u, s % NC, a, s // NC] = value[:, s * SH : (s + 1) * SH]

    def s0(u):
        y_wait(yx_copy, u)
        rows = xr[u].reshape(ROWS, W)
        partial(u, 0, dot(rows, wg[...]))
        partial(u, 1, dot(rows, wu[...]))
        y_wait(ys_copy, u)
        partial(u, 2, dot_nt(sr[u].reshape(ROWS, W), wd[...]))
        c1_copy(u).start()

    def s1(u):
        c1_copy(u).wait_recv()
        for j in (2, 1, 3, 0):
            xx = col(j)
            for a in range(3):
                value = (hp[u, core, a, xx].astype(F32) + cr[u, a, xx].astype(F32)).astype(BF16)
                q[u, j, 0, a] = value[:HALF]
                q[u, j, 1, a] = value[HALF:]
            if j == 2:
                x1_copy(u, 0).start()
                x1_copy(u, 1).start()
            elif j == 1:
                x1_copy(u, 2).start()
            elif j == 3:
                x1_copy(u, 3).start()

    def s2(u):
        for n, (j, half) in enumerate(((1, 0), (3, 1))):
            x1_copy(u, n).wait_recv()
            q[u, j, half] = (q[u, j, half].astype(F32) + t1[u, n].astype(F32)).astype(BF16)
            x2_copy(u, n).start()

    def s3(u):
        x1_copy(u, 2).wait_recv()
        x1_copy(u, 3).wait_recv()
        x2_copy(u, 0).wait_recv()
        x2_copy(u, 1).wait_recv()
        for half in range(2):
            h = q[u, 0, half].astype(F32) + t2[u, 0, half].astype(F32) + t2[u, 1, half].astype(F32)
            h_gate, h_up, d_act = h[0], h[1], h[2]
            sigma = 1.0 / (1.0 + jnp.exp(-h_gate))
            gb[u, core, x, half, 0] = (h_gate * sigma * h_up).astype(BF16)
            gb[u, core, x, half, 1] = (d_act * h_up * sigma * (1.0 + h_gate * (1.0 - sigma))).astype(BF16)
            gb[u, core, x, half, 2] = (d_act * h_gate * sigma).astype(BF16)
        ag_send(u, 0).start()
        ag_send(u, 1).start()
        cg_send(u, 0).start()

    def s4(u):
        ag_wait(u, 0)
        ag_send(u, 2).start()
        ag_wait(u, 1)
        ag_send(u, 3).start()
        cg_send(u, 1).start()
        cg_send(u, 2).start()

    def s5(u):
        ag_wait(u, 2)
        ag_wait(u, 3)
        cg_send(u, 3).start()

    def hidden(u, a):
        return jnp.concatenate(
            [gb[u, s % NC, s // NC, :, a].reshape(ROWS, SH) for s in range(NX * NC)], axis=1
        )

    def s6(u):
        for n in range(4):
            cg_wait(u, n)
        value = (dot_nt(hidden(u, 1), wg[...]) + dot_nt(hidden(u, 2), wu[...])).astype(BF16)
        cs[u, 0] = value[:HALF]
        cs[u, 1] = value[HALF:]
        c, h = u // 2, lax.rem(u, 2)

        @pl.when(h == 0)
        def _():
            yr[u, 0] = value[:HALF]
            ret_copy(c, 1).start()

        @pl.when(h == 1)
        def _():
            ret_copy(c, 2).start()
            ret_copy(c, 3).start()

    def s7(c):
        for k in (1, 2, 3):
            ret_copy(c, k).wait_recv()
        rows = yr[2 * c : 2 * c + 2].reshape(2 * ROWS, W)
        value = dot_tn(p2[c], rows).astype(BF16)
        for i in range(2):
            if PAIRS[c][i] == 0:
                zr[c, i] = value[i * T : (i + 1) * T]
            else:
                zs[c, i] = value[i * T : (i + 1) * T]
                zr_copy(c, i).start()

    def step(s, carry):
        for k, stage in ((5, s5), (4, s4), (3, s3), (2, s2), (1, s1)):

            @pl.when((s >= k) & (s < NU + k))
            def _(k=k, stage=stage):
                stage(s - k)

        @pl.when(s < NU)
        def _():
            s0(s)

        @pl.when((s >= DEPTH) & (s < NU + DEPTH))
        def _():
            s6(s - DEPTH)

        for c in range(NCH - 1):

            @pl.when(s == 2 * c + DEPTH + 2)
            def _(c=c):
                s7(c)

        @pl.when(s == 0)
        def _():
            pass_on(zx_copy, 2)
            pass_on(zd_copy, 2)

        @pl.when(s == 1)
        def _():
            pass_on(zx_copy, 3)
            pass_on(zd_copy, 3)

        @pl.when(s == 2)
        def _():
            zx_copy(4).wait_recv()
            zd_copy(-4).wait_recv()

        for c in range(1, NCH):

            @pl.when(s == 2 * c - 1)
            def _(c=c):
                place_x(c)
                place_s(c)

        return carry

    lax.fori_loop(0, NU + DEPTH, step, 0)

    everything = xr[...].reshape(NU * ROWS, W)
    for n in range(W // 128):
        xt[n * 128 : (n + 1) * 128] = everything[:, n * 128 : (n + 1) * 128].T

    def all_rows(xx, a):
        return jnp.concatenate(
            [gb[:, cc, xx, :, a].reshape(NU * ROWS, SH) for cc in range(NC)], axis=1
        )

    def gate_step(xx, carry):
        at = pl.ds(pl.multiple_of(xx * 2 * SH, 2 * SH), 2 * SH)
        gg[:, at] = dot(xt[...], all_rows(xx, 1)).astype(BF16)
        return carry

    lax.fori_loop(0, NX, gate_step, 0)
    outs = [
        pltpu.make_async_copy(src, dst, o_sem.at[n])
        for n, (src, dst) in enumerate(((gg, gg_hbm), (ug, ug_hbm), (dg, dg_hbm)))
    ]
    outs[0].start()
    s7(NCH - 1)

    def rest_step(xx, carry):
        at = pl.ds(pl.multiple_of(xx * 2 * SH, 2 * SH), 2 * SH)
        ug[:, at] = dot(xt[...], all_rows(xx, 2)).astype(BF16)
        dg[at, :] = dot_tn(all_rows(xx, 0), sr[...].reshape(NU * ROWS, W)).astype(BF16)
        return carry

    lax.fori_loop(0, NX, rest_step, 0)
    outs[1].start()
    outs[2].start()

    total = zr[0, 0].astype(F32)
    for c in range(NCH):
        for i in range(2):
            if PAIRS[c][i] != 0:
                zr_copy(c, i).wait_recv()
                total = total + zr[c, i].astype(F32)
    tg_ref[...] = total.astype(BF16)

    for off in range(1, NZ):
        info_copy(off).wait_send()
    for d in (1, 2, 3):
        for off in (d, -d):
            zx_copy(off).wait_send()
            zd_copy(off).wait_send()
    zx_copy(4).wait_send()
    zd_copy(-4).wait_send()

    def drain_u(u, carry):
        c1_copy(u).wait_send()
        for n in range(4):
            x1_copy(u, n).wait_send()
            ag_send(u, n).wait_send()
            cg_send(u, n).wait_send()
        for n in range(2):
            x2_copy(u, n).wait_send()
        return carry

    def drain_c(c, carry):
        for k in (1, 2, 3):
            yx_copy(c, k).wait_send()
            ys_copy(c, k).wait_send()
            ret_copy(c, k).wait_send()
        return carry

    lax.fori_loop(0, NU, drain_u, 0)
    lax.fori_loop(0, NCH, drain_c, 0)
    for c in range(NCH):
        for i in range(2):
            if PAIRS[c][i] != 0:
                zr_copy(c, i).wait_send()
    for copy in outs:
        copy.wait()


def on_device(tokens, cotangent, routes, gate_values, w_gate, w_up, w_down):
    pad = ((0, 2), (0, 0))
    ids = jnp.pad(routes.astype(F32).T, pad, constant_values=-1.0)
    info = jnp.concatenate([ids, jnp.pad(gate_values.T, pad)], axis=0)
    sem = pltpu.SemaphoreType.DMA

    def vm(*shape, dtype=BF16):
        return pltpu.VMEM(shape, dtype)

    vmem = pl.BlockSpec(memory_space=pltpu.VMEM)
    hbm = pl.BlockSpec(memory_space=pl.ANY)
    scratch = [
        vm(W, FF), vm(W, FF), vm(FF, W),
        vm(W, FF), vm(W, FF), vm(FF, W),
        vm(NZ, 16, T, dtype=F32), vm(NCH, 2, T, W), vm(NCH, 2, T, W),
        vm(NCH, 2 * ROWS, 2 * T), vm(NCH, 2 * ROWS, 1, dtype=F32),
        vm(NCH, 3, HALF, W), vm(NCH, 3, HALF, W),
        vm(NU, 2, HALF, W), vm(NU, 2, HALF, W),
        vm(NU, NC, 3, NX, ROWS, SH), vm(NU, 3, NX, ROWS, SH),
        vm(NU, NX, 2, 3, HALF, SH), vm(NU, 2, 3, HALF, SH), vm(NU, 2, 2, 3, HALF, SH),
        vm(NU, NC, NX, 2, 3, HALF, SH),
        vm(NU, 2, HALF, W), vm(NU, 2, HALF, W),
        vm(NCH, 2, T, W), vm(NCH, 2, T, W),
        vm(W, NU * ROWS),
    ]
    sems = []
    for shape in ((NZ,), (NZ,), (NZ,), (NCH, 4), (NCH, 4), (NU,), (NU, 4), (NU, 2), (NU, 4), (NU, 4), (NCH, 4), (NCH, 2)):
        sems += [sem(shape), sem(shape)]
    sems += [sem((3,)), sem((3,))]
    flops = 2 * NU * ROWS * W * FF * 8
    token_grad, gate_grad, up_grad, down_grad = pl.pallas_call(
        kernel,
        out_shape=(
            jax.ShapeDtypeStruct((T, W), BF16),
            jax.ShapeDtypeStruct((W, FF), BF16),
            jax.ShapeDtypeStruct((W, FF), BF16),
            jax.ShapeDtypeStruct((FF, W), BF16),
        ),
        in_specs=[vmem, vmem, vmem, hbm, hbm, hbm],
        out_specs=(vmem, hbm, hbm, hbm),
        scratch_shapes=scratch + sems,
        compiler_params=pltpu.CompilerParams(
            collective_id=0, has_side_effects=True, vmem_limit_bytes=60 * 1024 * 1024
        ),
        cost_estimate=pl.CostEstimate(flops=flops, bytes_accessed=12_000_000, transcendentals=0),
    )(tokens, cotangent, info, w_gate[0], w_up[0], w_down[0])
    return (token_grad, gate_grad[None], up_grad[None], down_grad[None])


def solution(mesh):
    return jax.shard_map(
        on_device,
        mesh=mesh,
        in_specs=(
            P("tok", "exp"),
            P("tok", "exp"),
            P("tok", None),
            P("tok", None),
            P("tok", "exp", None),
            P("tok", "exp", None),
            P("tok", None, "exp"),
        ),
        out_specs=(
            P("tok", "exp"),
            P("tok", "exp", None),
            P("tok", "exp", None),
            P("tok", None, "exp"),
        ),
        check_vma=False,
    )
```

```python
import jax
import jax.numpy as jnp
from jax import lax
from jax.experimental import pallas as pl
from jax.experimental.pallas import tpu as pltpu
from jax.sharding import PartitionSpec as P

MESH = pl.DeviceIdType.MESH
F32, BF16 = jnp.float32, jnp.bfloat16

NY, NZ, NX, NC = 4, 8, 4, 2
T = 128
CAP = 40
W = 640
FF = 1024
SH = FF // (NX * NC)
ORDER = (0, 1, 2, -3, 4, 3, -2, -1)
PART = {off: u for u, off in enumerate(ORDER)}
YOFF = (0, 1, -1, 2)
YINV = (0, 2, 1, 3)
NU = len(ORDER)
ROWS = NY * CAP
HALF = ROWS // 2
PAD = 48
DEPTH = 6


def dot(a, b):
    return jnp.dot(a, b, preferred_element_type=F32)


def dot_nt(a, b):
    return lax.dot_general(a, b, (((1,), (1,)), ((), ())), preferred_element_type=F32)


def dot_tn(a, b):
    return lax.dot_general(a, b, (((0,), (0,)), ((), ())), preferred_element_type=F32)


def kernel(
    tok_hbm, cot_hbm, ids_hbm, vals_hbm, wg_hbm, wu_hbm, wd_hbm,
    tg_ref, gg, ug, dg,
    wg, wu, wd, ids, vals, infob, zx, zd, pt, grow,
    ys, xsr, xr, sr, hp, cr, t1, t2, gb, rs, rr, zs, zr, own, xt,
    info_s, zx_s, zd_s, zr_s, ys_s, rs_s, xa_s, xb_s,
    info_r, zx_r, zd_r, zr_r, ys_r, rs_r, c1_r, t1_r, t2_r, ag_r, af_r, cg_r, in_sem,
):
    tok = lax.axis_index("tok")
    exp = lax.axis_index("exp")
    y, z = tok // NZ, lax.rem(tok, NZ)
    x, core = exp // NC, lax.rem(exp, NC)

    def at_z(off):
        return (y * NZ + lax.rem(z + off + NZ, NZ), exp)

    def at_y(off):
        return (lax.rem(y + off + NY, NY) * NZ + z, exp)

    def col(off):
        return lax.rem(x + off + NX, NX)

    def at_x(off):
        return (tok, col(off) * NC + core)

    sibling = (tok, x * NC + (1 - core))

    def rc(src, dst, s, r, dev):
        return pltpu.make_async_remote_copy(
            src_ref=src, dst_ref=dst, send_sem=s, recv_sem=r, device_id=dev, device_id_type=MESH
        )

    def bytes_of(ref, sem):
        pltpu.make_async_copy(ref, ref, sem).wait()

    def ring_copy(buf, ss, rs_, off):
        step = 1 if off > 0 else -1
        k = off % NZ
        return rc(buf.at[(off - step) % NZ], buf.at[k], ss.at[0], rs_.at[k], at_z(-step))

    def info_copy(off):
        return ring_copy(infob, info_s, info_r, off)

    def zx_copy(off):
        return ring_copy(zx, zx_s, zx_r, off)

    def zd_copy(off):
        return ring_copy(zd, zd_s, zd_r, off)

    def zr_copy(off):
        k = off % NZ - 1
        return rc(zs.at[k], zr.at[k], zr_s.at[0], zr_r.at[k], at_z(1 if off == 4 else off))

    def ys_copy(u, k):
        return rc(ys.at[u, k - 1], xsr.at[u, YINV[k]], ys_s.at[u], ys_r.at[u], at_y(YOFF[k]))

    def rs_copy(u, k):
        return rc(rs.at[u, k - 1], rr.at[u, YINV[k]], rs_s.at[u], rs_r.at[u], at_y(YOFF[k]))

    def c1_copy(u):
        return rc(hp.at[u, 1 - core], cr.at[u], xa_s.at[u], c1_r.at[u], sibling)

    def x1_copy(u, n):
        src, dst, r, to = (
            (hp.at[u, core, col(2), 0], t1.at[u, 0], t1_r, 1),
            (hp.at[u, core, col(2), 1], t1.at[u, 1], t1_r, -1),
            (hp.at[u, core, col(1), 1], t2.at[u, 0, 1], t2_r, 1),
            (hp.at[u, core, col(-1), 0], t2.at[u, 1, 0], t2_r, -1),
            (hp.at[u, core, col(1), 0], t2.at[u, 0, 0], t2_r, 1),
            (hp.at[u, core, col(-1), 1], t2.at[u, 1, 1], t2_r, -1),
        )[n]
        return rc(src, dst, xb_s.at[u], r.at[u], at_x(to))

    def ag_send(u, n):
        part, r, to = (
            (gb.at[u, core, x], ag_r.at[u, 0], 1),
            (gb.at[u, core, x], ag_r.at[u, 1], -1),
            (gb.at[u, core, col(-1), 0], af_r.at[u], 1),
            (gb.at[u, core, col(1), 1], af_r.at[u], -1),
        )[n]
        return rc(part, part, xb_s.at[u], r, at_x(to))

    def cg_send(u, off):
        part = gb.at[u, core, col(off)]
        return rc(part, part, xa_s.at[u], cg_r.at[u], sibling)

    inputs = [
        pltpu.make_async_copy(src, dst, in_sem.at[n])
        for n, (src, dst) in enumerate(
            (
                (ids_hbm, ids),
                (vals_hbm, vals),
                (tok_hbm, zx.at[0]),
                (cot_hbm, zd.at[0]),
                (wg_hbm, wg),
                (wu_hbm, wu),
                (wd_hbm, wd),
            )
        )
    ]

    def make_tables(u):
        before = (
            lax.broadcasted_iota(jnp.int32, (T, T), 0) < lax.broadcasted_iota(jnp.int32, (T, T), 1)
        ).astype(BF16)
        block = infob[ORDER[u] % NZ]
        named, value = block[0:8], block[8:16]
        masks, gates = [], []
        for k in range(NY):
            expert = (lax.rem(y + YOFF[k] + NY, NY) * NZ + z).astype(F32)
            hit = named == expert
            masks.append(jnp.sum(jnp.where(hit, 1.0, 0.0), axis=0, keepdims=True))
            gates.append(jnp.sum(jnp.where(hit, value, 0.0), axis=0, keepdims=True))
        mask_all = jnp.concatenate(masks + [jnp.zeros((8 - NY, T), F32)], axis=0)
        rank_all = dot(mask_all.astype(BF16), before)
        want = lax.broadcasted_iota(jnp.int32, (CAP, T), 0).astype(F32)
        tables, gcols = [], []
        for k in range(NY):
            on = (rank_all[k : k + 1] == want) & (mask_all[k : k + 1] > 0.5)
            tables.append(jnp.where(on, 1.0, 0.0))
            gcols.append(jnp.sum(jnp.where(on, gates[k], 0.0), axis=1, keepdims=True))
        pt[u] = jnp.concatenate(tables, axis=0).astype(BF16)
        grow[u] = jnp.concatenate(gcols, axis=0)

    def enter():
        barrier = pltpu.get_barrier_semaphore()
        partners = [at_z(off) for off in (1, -1, 2, -2, 3, -3)]
        partners += [at_y(off) for off in (1, -1, 2)] + [at_x(1), at_x(-1), sibling]
        for dev in partners:
            pl.semaphore_signal(barrier, inc=1, device_id=dev, device_id_type=MESH)
        for copy in inputs:
            copy.start()
        for copy in inputs[:4]:
            copy.wait()
        nought = jnp.zeros((2, T), F32)
        infob[0] = jnp.concatenate([ids[...].astype(F32), nought - 1.0, vals[...], nought], axis=0)
        make_tables(0)
        gather(0)
        pl.semaphore_wait(barrier, len(partners))

    def gather(u):
        k = ORDER[u] % NZ
        xs = dot(pt[u], zx[k])
        ss = dot(pt[u], zd[k]) * grow[u]
        for k in range(NY):
            both = jnp.concatenate([xs[k * CAP : (k + 1) * CAP], ss[k * CAP : (k + 1) * CAP]], axis=0)
            if k == 0:
                xsr[u, 0] = both.astype(BF16)
            else:
                ys[u, k - 1] = both.astype(BF16)

    def send_rows(u):
        for k in (3, 1, 2):
            ys_copy(u, k).start()

    def place(u):
        make_tables(u)
        gather(u)
        send_rows(u)

    def pass_x(d):
        for off in (d, -d):
            info_copy(off).wait_recv()
            zx_copy(off).wait_recv()
            if d < 3 or off > 0:
                after = off + (1 if off > 0 else -1)
                info_copy(after).start()
                zx_copy(after).start()

    def pass_d(d):
        for off in (d, -d):
            zd_copy(off).wait_recv()
            if d < 3 or off < 0:
                zd_copy(off + (1 if off > 0 else -1)).start()

    def partial(u, a, value):
        value = value.astype(BF16)
        for s in range(NX * NC):
            hp[u, s % NC, s // NC, :, a] = value[:, s * SH : (s + 1) * SH].reshape(2, HALF, SH)

    def s0(u):
        bytes_of(xsr.at[u, 1:NY], ys_r.at[u])
        both = [xsr[u, j].astype(F32) for j in range(NY)]
        rows = jnp.concatenate([v[:CAP] for v in both], axis=0).astype(BF16)
        scaled = jnp.concatenate([v[CAP:] for v in both], axis=0).astype(BF16)
        xr[u] = rows
        sr[u] = scaled
        partial(u, 0, dot(rows, wg[...]))
        partial(u, 1, dot(rows, wu[...]))
        partial(u, 2, dot_nt(scaled, wd[...]))
        c1_copy(u).start()

    def s1(u):
        c1_copy(u).wait_recv()
        for off in (2, 1, -1, 0):
            xx = col(off)
            hp[u, core, xx] = (hp[u, core, xx].astype(F32) + cr[u, xx].astype(F32)).astype(BF16)
            for n in {2: (0, 1), 1: (2,), -1: (3,), 0: ()}[off]:
                x1_copy(u, n).start()

    def s2(u):
        bytes_of(t1.at[u], t1_r.at[u])
        for n, (off, half) in enumerate(((1, 0), (-1, 1))):
            xx = col(off)
            hp[u, core, xx, half] = (hp[u, core, xx, half].astype(F32) + t1[u, n].astype(F32)).astype(BF16)
            x1_copy(u, 4 + n).start()

    def s3(u):
        bytes_of(t2.at[u], t2_r.at[u])
        for half in range(2):
            h = hp[u, core, x, half].astype(F32) + t2[u, 0, half].astype(F32) + t2[u, 1, half].astype(F32)
            h_gate, h_up, d_act = h[0], h[1], h[2]
            sigma = 1.0 / (1.0 + jnp.exp(-h_gate))
            gb[u, core, x, half, 0] = (h_gate * sigma * h_up).astype(BF16)
            gb[u, core, x, half, 1] = (d_act * h_up * sigma * (1.0 + h_gate * (1.0 - sigma))).astype(BF16)
            gb[u, core, x, half, 2] = (d_act * h_gate * sigma).astype(BF16)
        ag_send(u, 0).start()
        ag_send(u, 1).start()
        cg_send(u, 0).start()

    def s4(u):
        bytes_of(gb.at[u, core, col(-1)], ag_r.at[u, 0])
        ag_send(u, 2).start()
        bytes_of(gb.at[u, core, col(1)], ag_r.at[u, 1])
        ag_send(u, 3).start()
        cg_send(u, -1).start()
        cg_send(u, 1).start()

    def s5(u):
        bytes_of(gb.at[u, core, col(2)], af_r.at[u])
        cg_send(u, 2).start()

    def hidden(u, a):
        return jnp.concatenate(
            [gb[u, s % NC, s // NC, :, a].reshape(ROWS, SH) for s in range(NX * NC)], axis=1
        )

    def s6(u):
        bytes_of(gb.at[u, 1 - core], cg_r.at[u])
        value = dot_nt(hidden(u, 1), wg[...]) + dot_nt(hidden(u, 2), wu[...])
        nought = jnp.zeros((PAD - CAP, W), F32)
        for k in (3, 1, 2, 0):
            slot = jnp.concatenate([value[k * CAP : (k + 1) * CAP], nought], axis=0).astype(BF16)
            if k == 0:
                rr[u, 0] = slot
            else:
                rs[u, k - 1] = slot
                rs_copy(u, k).start()

    def sent_u(u):
        bytes_of(hp.at[u], xa_s.at[u])
        bytes_of(hp.at[u, :, 0:3], xb_s.at[u])
        bytes_of(ys.at[u], ys_s.at[u])

    def sent_z():
        bytes_of(infob.at[0 : NZ - 1], info_s.at[0])
        bytes_of(zx.at[0 : NZ - 1], zx_s.at[0])
        bytes_of(zd.at[0 : NZ - 1], zd_s.at[0])

    def s7(u):
        bytes_of(rr.at[u, 1:NY], rs_r.at[u])
        rows = jnp.concatenate([rr[u, j].astype(F32)[:CAP] for j in range(NY)], axis=0).astype(BF16)
        value = dot_tn(pt[u], rows)
        if ORDER[u] == 0:
            own[...] = value
        else:
            zs[ORDER[u] % NZ - 1] = value.astype(BF16)
            if ORDER[u] != 3:
                zr_copy(ORDER[u]).start()

    def join():
        zr_copy(4).wait_recv()
        zs[2] = (zs[2].astype(F32) + zr[3].astype(F32)).astype(BF16)
        zr_copy(3).start()

    def step(s, carry):
        for k, stage, first in ((1, s1, 2), (5, s5, 0), (4, s4, 1), (3, s3, 1), (2, s2, 1)):

            @pl.when((s >= k + first) & (s < NU + k))
            def _(k=k, stage=stage):
                stage(s - k)

        @pl.when(s < NU)
        def _():
            s0(s)

        @pl.when((s >= DEPTH) & (s < NU + DEPTH))
        def _():
            s6(s - DEPTH)
            sent_u(s - DEPTH)

        for u in range(NU - 1):

            @pl.when(s == u + DEPTH + 1)
            def _(u=u):
                s7(u)

        for u in range(5, NU):

            @pl.when(s == u - 2)
            def _(u=u):
                place(u)

        @pl.when(s == NU)
        def _():
            sent_z()

        return carry

    enter()
    for off in (1, -1):
        info_copy(off).start()
    for off in (1, -1):
        zx_copy(off).start()
    send_rows(0)
    for off in (1, -1):
        zd_copy(off).start()
    for copy in inputs[4:]:
        copy.wait()
    s0(0)
    pass_x(1)
    pass_d(1)
    place(1)
    s1(0)
    pass_x(2)
    s2(0)
    pass_d(2)
    place(2)
    s3(0)
    s0(1)
    pass_x(3)
    s1(1)
    s4(0)
    pass_d(3)
    place(3)
    s0(2)
    info_copy(4).wait_recv()
    zx_copy(4).wait_recv()
    zd_copy(-4).wait_recv()
    place(4)
    lax.fori_loop(3, NU + DEPTH, step, 0)

    everything = xr[...].reshape(NU * ROWS, W)
    for n in range(W // 128):
        xt[n * 128 : (n + 1) * 128] = everything[:, n * 128 : (n + 1) * 128].T

    def all_rows(xx, a):
        return jnp.concatenate(
            [gb[:, cc, xx, :, a].reshape(NU * ROWS, SH) for cc in range(NC)], axis=1
        )

    def gate_step(xx, carry):
        at = pl.ds(pl.multiple_of(xx * 2 * SH, 2 * SH), 2 * SH)
        gg[:, at] = dot(xt[...], all_rows(xx, 1)).astype(BF16)
        return carry

    join()
    lax.fori_loop(0, NX, gate_step, 0)
    s7(NU - 1)

    def rest_step(xx, carry):
        at = pl.ds(pl.multiple_of(xx * 2 * SH, 2 * SH), 2 * SH)
        ug[:, at] = dot(xt[...], all_rows(xx, 2)).astype(BF16)
        dg[at, :] = dot_tn(all_rows(xx, 0), sr[...].reshape(NU * ROWS, W)).astype(BF16)
        return carry

    lax.fori_loop(0, NX, rest_step, 0)

    def finish():
        total = own[...]
        for off in (1, 2, -3, 3, -2, -1):
            zr_copy(off).wait_recv()
            total = total + zr[off % NZ - 1].astype(F32)
        tg_ref[...] = total.astype(BF16)
        bytes_of(zs, zr_s.at[0])
        for u in range(NU):
            bytes_of(rs.at[u], rs_s.at[u])

    finish()


def write_out(*refs):
    srcs, dsts, done = refs[:4], refs[4:8], refs[8]
    copies = [pltpu.make_async_copy(srcs[n], dsts[n], done.at[n]) for n in range(4)]
    for copy in copies:
        copy.start()
    for copy in copies:
        copy.wait()


def on_device(tokens, cotangent, routes, gate_values, w_gate, w_up, w_down):
    sem = pltpu.SemaphoreType.DMA

    def vm(*shape, dtype=BF16):
        return pltpu.VMEM(shape, dtype)

    vmem = pl.BlockSpec(memory_space=pltpu.VMEM)
    hbm = pl.BlockSpec(memory_space=pl.ANY)
    scratch = [
        vm(W, FF), vm(W, FF), vm(FF, W),
        vm(6, T, dtype=jnp.int32), vm(6, T, dtype=F32), vm(NZ, 16, T, dtype=F32),
        vm(NZ, T, W), vm(NZ, T, W),
        vm(NU, ROWS, T), vm(NU, ROWS, 1, dtype=F32),
        vm(NU, 3, 2 * CAP, W), vm(NU, NY, 2 * CAP, W),
        vm(NU, ROWS, W), vm(NU, ROWS, W),
        vm(NU, NC, NX, 2, 3, HALF, SH), vm(NU, NX, 2, 3, HALF, SH),
        vm(NU, 2, 3, HALF, SH), vm(NU, 2, 2, 3, HALF, SH),
        vm(NU, NC, NX, 2, 3, HALF, SH),
        vm(NU, 3, PAD, W), vm(NU, NY, PAD, W),
        vm(NZ - 1, T, W), vm(NZ - 1, T, W), vm(T, W, dtype=F32),
        vm(W, NU * ROWS),
    ]
    sems = [sem((1,)) for _ in range(4)]
    sems += [sem((NU,)) for _ in range(4)]
    sems += [sem((NZ,)), sem((NZ,)), sem((NZ,)), sem((NZ - 1,))]
    sems += [sem((NU,)) for _ in range(5)]
    sems += [sem((NU, 2)), sem((NU,)), sem((NU,)), sem((7,))]
    flops = 2 * NU * ROWS * W * FF * 8
    shapes = ((T, W), (W, FF), (W, FF), (FF, W))
    results = pl.pallas_call(
        kernel,
        out_shape=tuple(pltpu.VMEM(shape, BF16) for shape in shapes),
        in_specs=[pl.BlockSpec(memory_space=pltpu.HBM)] * 7,
        out_specs=(vmem, vmem, vmem, vmem),
        scratch_shapes=scratch + sems,
        compiler_params=pltpu.CompilerParams(
            collective_id=0, has_side_effects=True, vmem_limit_bytes=50 * 1024 * 1024
        ),
        cost_estimate=pl.CostEstimate(flops=flops, bytes_accessed=12_000_000, transcendentals=0),
    )(tokens, cotangent, routes.T, gate_values.T, w_gate[0], w_up[0], w_down[0])
    token_grad, gate_grad, up_grad, down_grad = pl.pallas_call(
        write_out,
        out_shape=tuple(jax.ShapeDtypeStruct(shape, BF16) for shape in shapes),
        in_specs=[hbm] * 4,
        out_specs=(hbm,) * 4,
        scratch_shapes=[sem((4,))],
        compiler_params=pltpu.CompilerParams(vmem_limit_bytes=1024 * 1024),
    )(*(pltpu.with_memory_space_constraint(r, pltpu.VMEM) for r in results))
    return (token_grad, gate_grad[None], up_grad[None], down_grad[None])


def solution(mesh):
    return jax.shard_map(
        on_device,
        mesh=mesh,
        in_specs=(
            P("tok", "exp"),
            P("tok", "exp"),
            P("tok", None),
            P("tok", None),
            P("tok", "exp", None),
            P("tok", "exp", None),
            P("tok", None, "exp"),
        ),
        out_specs=(
            P("tok", "exp"),
            P("tok", "exp", None),
            P("tok", "exp", None),
            P("tok", None, "exp"),
        ),
        check_vma=False,
    )
```

```python
import jax
import jax.numpy as jnp
from jax import lax
from jax.experimental import pallas as pl
from jax.experimental.pallas import tpu as pltpu
from jax.sharding import PartitionSpec as P

MESH = pl.DeviceIdType.MESH
F32, BF16 = jnp.float32, jnp.bfloat16

NY, NZ, NX, NC = 4, 8, 4, 2
T = 128
CAP = 40
W = 640
FF = 1024
SH = FF // (NX * NC)
ORDER = (0, 1, 2, -3, 4, 3, -2, -1)
PART = {off: u for u, off in enumerate(ORDER)}
YOFF = (0, 1, -1, 2)
YINV = (0, 2, 1, 3)
NU = len(ORDER)
ROWS = NY * CAP
HALF = ROWS // 2
PAD = 48
DEPTH = 6


def dot(a, b):
    return jnp.dot(a, b, preferred_element_type=F32)


def dot_nt(a, b):
    return lax.dot_general(a, b, (((1,), (1,)), ((), ())), preferred_element_type=F32)


def dot_tn(a, b):
    return lax.dot_general(a, b, (((0,), (0,)), ((), ())), preferred_element_type=F32)


def kernel(
    tok_hbm, cot_hbm, ids_hbm, vals_hbm, wg_hbm, wu_hbm, wd_hbm,
    tg_ref, gg, ug, dg,
    wg, wu, wd, ids, vals, infob, zx, zd, pt, grow,
    ys, xsr, xr, sr, hp, cr, t1, t2, gb, rs, rr, zs, zr, own, xt,
    info_s, zx_s, zd_s, zr_s, ys_s, rs_s, xa_s, xb_s,
    info_r, zx_r, zd_r, zr_r, ys_r, rs_r, c1_r, t1_r, t2_r, ag_r, af_r, cg_r, in_sem,
):
    tok = lax.axis_index("tok")
    exp = lax.axis_index("exp")
    y, z = tok // NZ, lax.rem(tok, NZ)
    x, core = exp // NC, lax.rem(exp, NC)

    def at_z(off):
        return (y * NZ + lax.rem(z + off + NZ, NZ), exp)

    def at_y(off):
        return (lax.rem(y + off + NY, NY) * NZ + z, exp)

    def col(off):
        return lax.rem(x + off + NX, NX)

    def at_x(off):
        return (tok, col(off) * NC + core)

    sibling = (tok, x * NC + (1 - core))

    def rc(src, dst, s, r, dev):
        return pltpu.make_async_remote_copy(
            src_ref=src, dst_ref=dst, send_sem=s, recv_sem=r, device_id=dev, device_id_type=MESH
        )

    def bytes_of(ref, sem):
        pltpu.make_async_copy(ref, ref, sem).wait()

    def ring_copy(buf, ss, rs_, off):
        step = 1 if off > 0 else -1
        k = off % NZ
        return rc(buf.at[(off - step) % NZ], buf.at[k], ss.at[0], rs_.at[k], at_z(-step))

    def info_copy(off):
        return ring_copy(infob, info_s, info_r, off)

    def zx_copy(off):
        return ring_copy(zx, zx_s, zx_r, off)

    def zd_copy(off):
        return ring_copy(zd, zd_s, zd_r, off)

    def zr_copy(off):
        k = off % NZ - 1
        return rc(zs.at[k], zr.at[k], zr_s.at[0], zr_r.at[k], at_z(1 if off == 4 else off))

    def ys_copy(u, k):
        return rc(ys.at[u, k - 1], xsr.at[u, YINV[k]], ys_s.at[u], ys_r.at[u], at_y(YOFF[k]))

    def rs_copy(u, k):
        return rc(rs.at[u, k - 1], rr.at[u, YINV[k]], rs_s.at[u], rs_r.at[u], at_y(YOFF[k]))

    def c1_copy(u):
        return rc(hp.at[u, 1 - core], cr.at[u], xa_s.at[u], c1_r.at[u], sibling)

    def x1_copy(u, n):
        src, dst, r, to = (
            (hp.at[u, core, col(2), 0], t1.at[u, 0], t1_r, 1),
            (hp.at[u, core, col(2), 1], t1.at[u, 1], t1_r, -1),
            (hp.at[u, core, col(1), 1], t2.at[u, 0, 1], t2_r, 1),
            (hp.at[u, core, col(-1), 0], t2.at[u, 1, 0], t2_r, -1),
            (hp.at[u, core, col(1), 0], t2.at[u, 0, 0], t2_r, 1),
            (hp.at[u, core, col(-1), 1], t2.at[u, 1, 1], t2_r, -1),
        )[n]
        return rc(src, dst, xb_s.at[u], r.at[u], at_x(to))

    def ag_send(u, n):
        part, r, to = (
            (gb.at[u, core, x], ag_r.at[u, 0], 1),
            (gb.at[u, core, x], ag_r.at[u, 1], -1),
            (gb.at[u, core, col(-1), 0], af_r.at[u], 1),
            (gb.at[u, core, col(1), 1], af_r.at[u], -1),
        )[n]
        return rc(part, part, xb_s.at[u], r, at_x(to))

    def cg_send(u, off):
        part = gb.at[u, core, col(off)]
        return rc(part, part, xa_s.at[u], cg_r.at[u], sibling)

    inputs = [
        pltpu.make_async_copy(src, dst, in_sem.at[n])
        for n, (src, dst) in enumerate(
            (
                (ids_hbm, ids),
                (vals_hbm, vals),
                (tok_hbm, zx.at[0]),
                (cot_hbm, zd.at[0]),
                (wg_hbm, wg),
                (wu_hbm, wu),
                (wd_hbm, wd),
            )
        )
    ]

    def make_tables(u):
        before = (
            lax.broadcasted_iota(jnp.int32, (T, T), 0) < lax.broadcasted_iota(jnp.int32, (T, T), 1)
        ).astype(BF16)
        block = infob[ORDER[u] % NZ]
        named, value = block[0:8], block[8:16]
        masks, gates = [], []
        for k in range(NY):
            expert = (lax.rem(y + YOFF[k] + NY, NY) * NZ + z).astype(F32)
            hit = named == expert
            masks.append(jnp.sum(jnp.where(hit, 1.0, 0.0), axis=0, keepdims=True))
            gates.append(jnp.sum(jnp.where(hit, value, 0.0), axis=0, keepdims=True))
        mask_all = jnp.concatenate(masks + [jnp.zeros((8 - NY, T), F32)], axis=0)
        rank_all = dot(mask_all.astype(BF16), before)
        want = lax.broadcasted_iota(jnp.int32, (CAP, T), 0).astype(F32)
        tables, gcols = [], []
        for k in range(NY):
            on = (rank_all[k : k + 1] == want) & (mask_all[k : k + 1] > 0.5)
            tables.append(jnp.where(on, 1.0, 0.0))
            gcols.append(jnp.sum(jnp.where(on, gates[k], 0.0), axis=1, keepdims=True))
        pt[u] = jnp.concatenate(tables, axis=0).astype(BF16)
        grow[u] = jnp.concatenate(gcols, axis=0)

    def enter():
        barrier = pltpu.get_barrier_semaphore()
        partners = [at_z(off) for off in (1, -1, 2, -2, 3, -3)]
        partners += [at_y(off) for off in (1, -1, 2)] + [at_x(1), at_x(-1), sibling]
        for dev in partners:
            pl.semaphore_signal(barrier, inc=1, device_id=dev, device_id_type=MESH)
        for copy in inputs:
            copy.start()
        for copy in inputs[:4]:
            copy.wait()
        nought = jnp.zeros((2, T), F32)
        infob[0] = jnp.concatenate([ids[...].astype(F32), nought - 1.0, vals[...], nought], axis=0)
        make_tables(0)
        gather(0)
        pl.semaphore_wait(barrier, len(partners))

    def gather(u):
        k = ORDER[u] % NZ
        xs = dot(pt[u], zx[k])
        ss = dot(pt[u], zd[k]) * grow[u]
        for k in range(NY):
            both = jnp.concatenate([xs[k * CAP : (k + 1) * CAP], ss[k * CAP : (k + 1) * CAP]], axis=0)
            if k == 0:
                xsr[u, 0] = both.astype(BF16)
            else:
                ys[u, k - 1] = both.astype(BF16)

    def send_rows(u):
        for k in (3, 1, 2):
            ys_copy(u, k).start()

    def place(u):
        make_tables(u)
        gather(u)
        send_rows(u)

    def pass_x(d):
        for off in (d, -d):
            info_copy(off).wait_recv()
            zx_copy(off).wait_recv()
            if d < 3 or off > 0:
                after = off + (1 if off > 0 else -1)
                info_copy(after).start()
                zx_copy(after).start()

    def pass_d(d):
        for off in (d, -d):
            zd_copy(off).wait_recv()
            if d < 3 or off < 0:
                zd_copy(off + (1 if off > 0 else -1)).start()

    def partial(u, a, value):
        value = value.astype(BF16)
        for s in range(NX * NC):
            hp[u, s % NC, s // NC, :, a] = value[:, s * SH : (s + 1) * SH].reshape(2, HALF, SH)

    def s0(u):
        bytes_of(xsr.at[u, 1:NY], ys_r.at[u])
        both = [xsr[u, j].astype(F32) for j in range(NY)]
        rows = jnp.concatenate([v[:CAP] for v in both], axis=0).astype(BF16)
        scaled = jnp.concatenate([v[CAP:] for v in both], axis=0).astype(BF16)
        xr[u] = rows
        sr[u] = scaled
        partial(u, 0, dot(rows, wg[...]))
        partial(u, 1, dot(rows, wu[...]))
        partial(u, 2, dot_nt(scaled, wd[...]))
        c1_copy(u).start()

    def s1(u):
        c1_copy(u).wait_recv()
        for off in (2, 1, -1, 0):
            xx = col(off)
            hp[u, core, xx] = (hp[u, core, xx].astype(F32) + cr[u, xx].astype(F32)).astype(BF16)
            for n in {2: (0, 1), 1: (2,), -1: (3,), 0: ()}[off]:
                x1_copy(u, n).start()

    def s2(u):
        bytes_of(t1.at[u], t1_r.at[u])
        for n, (off, half) in enumerate(((1, 0), (-1, 1))):
            xx = col(off)
            hp[u, core, xx, half] = (hp[u, core, xx, half].astype(F32) + t1[u, n].astype(F32)).astype(BF16)
            x1_copy(u, 4 + n).start()

    def s3(u):
        bytes_of(t2.at[u], t2_r.at[u])
        for half in range(2):
            h = hp[u, core, x, half].astype(F32) + t2[u, 0, half].astype(F32) + t2[u, 1, half].astype(F32)
            h_gate, h_up, d_act = h[0], h[1], h[2]
            sigma = 1.0 / (1.0 + jnp.exp(-h_gate))
            gb[u, core, x, half, 0] = (h_gate * sigma * h_up).astype(BF16)
            gb[u, core, x, half, 1] = (d_act * h_up * sigma * (1.0 + h_gate * (1.0 - sigma))).astype(BF16)
            gb[u, core, x, half, 2] = (d_act * h_gate * sigma).astype(BF16)
        ag_send(u, 0).start()
        ag_send(u, 1).start()
        cg_send(u, 0).start()

    def s4(u):
        bytes_of(gb.at[u, core, col(-1)], ag_r.at[u, 0])
        ag_send(u, 2).start()
        bytes_of(gb.at[u, core, col(1)], ag_r.at[u, 1])
        ag_send(u, 3).start()
        cg_send(u, -1).start()
        cg_send(u, 1).start()

    def s5(u):
        bytes_of(gb.at[u, core, col(2)], af_r.at[u])
        cg_send(u, 2).start()

    def hidden(u, a):
        return jnp.concatenate(
            [gb[u, s % NC, s // NC, :, a].reshape(ROWS, SH) for s in range(NX * NC)], axis=1
        )

    def s6(u):
        bytes_of(gb.at[u, 1 - core], cg_r.at[u])
        value = dot_nt(hidden(u, 1), wg[...]) + dot_nt(hidden(u, 2), wu[...])
        nought = jnp.zeros((PAD - CAP, W), F32)
        for k in (3, 1, 2, 0):
            slot = jnp.concatenate([value[k * CAP : (k + 1) * CAP], nought], axis=0).astype(BF16)
            if k == 0:
                rr[u, 0] = slot
            else:
                rs[u, k - 1] = slot
                rs_copy(u, k).start()

    def sent_u(u):
        bytes_of(hp.at[u], xa_s.at[u])
        bytes_of(hp.at[u, :, 0:3], xb_s.at[u])
        bytes_of(ys.at[u], ys_s.at[u])

    def sent_z():
        bytes_of(infob.at[0 : NZ - 1], info_s.at[0])
        bytes_of(zx.at[0 : NZ - 1], zx_s.at[0])
        bytes_of(zd.at[0 : NZ - 1], zd_s.at[0])

    def s7(u):
        bytes_of(rr.at[u, 1:NY], rs_r.at[u])
        rows = jnp.concatenate([rr[u, j].astype(F32)[:CAP] for j in range(NY)], axis=0).astype(BF16)
        value = dot_tn(pt[u], rows)
        if ORDER[u] == 0:
            own[...] = value
        else:
            zs[ORDER[u] % NZ - 1] = value.astype(BF16)
            if ORDER[u] != 3:
                zr_copy(ORDER[u]).start()

    def join():
        zr_copy(4).wait_recv()
        zs[2] = (zs[2].astype(F32) + zr[3].astype(F32)).astype(BF16)
        zr_copy(3).start()

    def step(s, carry):
        def each(stage, lag, first=0):
            @pl.when((s >= lag + first) & (s < NU + lag))
            def _():
                stage(s - lag)

        each(s1, 1)
        each(s5, 4)
        each(s4, 3, 1)
        each(s3, 2, 1)

        @pl.when(s == 3)
        def _():
            info_copy(4).wait_recv()
            zx_copy(4).wait_recv()
            zd_copy(-4).wait_recv()
            place(4)

        each(s0, 0)
        each(s2, 1)
        each(s6, 4)
        each(sent_u, 5)
        for u in range(4):

            @pl.when(s == u + 5)
            def _(u=u):
                s7(u)

        for u in range(5, NU):

            @pl.when(s == u - 2)
            def _(u=u):
                place(u)

        return carry

    enter()
    send_rows(0)
    for off in (1, -1):
        info_copy(off).start()
    for off in (1, -1):
        zx_copy(off).start()
    for off in (1, -1):
        zd_copy(off).start()
    for copy in inputs[4:]:
        copy.wait()
    s0(0)
    pass_x(1)
    pass_d(1)
    place(1)
    s1(0)
    s2(0)
    pass_x(2)
    pass_d(2)
    s3(0)
    s0(1)
    place(2)
    s1(1)
    s4(0)
    s2(1)
    pass_x(3)
    pass_d(3)
    place(3)
    s0(2)
    lax.fori_loop(3, NU + 1, step, 0)
    s5(5)
    s4(6)
    s3(7)
    s6(5)
    s7(4)
    s5(6)
    s4(7)
    s6(6)
    s7(5)
    s5(7)
    s6(7)
    sent_z()
    for u in range(4, NU):
        sent_u(u)
    join()
    s7(6)

    everything = xr[...].reshape(NU * ROWS, W)
    for n in range(W // 128):
        xt[n * 128 : (n + 1) * 128] = everything[:, n * 128 : (n + 1) * 128].T

    def all_rows(xx, a):
        return jnp.concatenate(
            [gb[:, cc, xx, :, a].reshape(NU * ROWS, SH) for cc in range(NC)], axis=1
        )

    def gate_step(xx, carry):
        at = pl.ds(pl.multiple_of(xx * 2 * SH, 2 * SH), 2 * SH)
        gg[:, at] = dot(xt[...], all_rows(xx, 1)).astype(BF16)
        return carry

    lax.fori_loop(0, NX, gate_step, 0)
    s7(7)

    def up_step(xx, carry):
        at = pl.ds(pl.multiple_of(xx * 2 * SH, 2 * SH), 2 * SH)
        ug[:, at] = dot(xt[...], all_rows(xx, 2)).astype(BF16)
        return carry

    lax.fori_loop(0, NX, up_step, 0)

    def down_step(xx, carry):
        at = pl.ds(pl.multiple_of(xx * 2 * SH, 2 * SH), 2 * SH)
        dg[at, :] = dot_tn(all_rows(xx, 0), sr[...].reshape(NU * ROWS, W)).astype(BF16)
        return carry

    lax.fori_loop(0, NX, down_step, 0)

    def finish():
        total = own[...]
        for off in (1, 2, -3, 3, -2, -1):
            zr_copy(off).wait_recv()
            total = total + zr[off % NZ - 1].astype(F32)
        tg_ref[...] = total.astype(BF16)
        bytes_of(zs, zr_s.at[0])
        for u in range(NU):
            bytes_of(rs.at[u], rs_s.at[u])

    finish()


def write_out(*refs):
    srcs, dsts, done = refs[:4], refs[4:8], refs[8]
    copies = []
    for src, dst in zip(srcs, dsts):
        for rows in range(0, src.shape[0], T):
            part = pl.ds(rows, T)
            copies.append(pltpu.make_async_copy(src.at[part], dst.at[part], done.at[len(copies)]))
    for copy in copies:
        copy.start()
    for copy in copies:
        copy.wait()


def hbm_of(array):
    return pltpu.with_memory_space_constraint(array, pltpu.HBM)


def on_device(tokens, cotangent, routes, gate_values, w_gate, w_up, w_down):
    sem = pltpu.SemaphoreType.DMA

    def vm(*shape, dtype=BF16):
        return pltpu.VMEM(shape, dtype)

    vmem = pl.BlockSpec(memory_space=pltpu.VMEM)
    hbm = pl.BlockSpec(memory_space=pl.ANY)
    scratch = [
        vm(W, FF), vm(W, FF), vm(FF, W),
        vm(6, T, dtype=jnp.int32), vm(6, T, dtype=F32), vm(NZ, 16, T, dtype=F32),
        vm(NZ, T, W), vm(NZ, T, W),
        vm(NU, ROWS, T), vm(NU, ROWS, 1, dtype=F32),
        vm(NU, 3, 2 * CAP, W), vm(NU, NY, 2 * CAP, W),
        vm(NU, ROWS, W), vm(NU, ROWS, W),
        vm(NU, NC, NX, 2, 3, HALF, SH), vm(NU, NX, 2, 3, HALF, SH),
        vm(NU, 2, 3, HALF, SH), vm(NU, 2, 2, 3, HALF, SH),
        vm(NU, NC, NX, 2, 3, HALF, SH),
        vm(NU, 3, PAD, W), vm(NU, NY, PAD, W),
        vm(NZ - 1, T, W), vm(NZ - 1, T, W), vm(T, W, dtype=F32),
        vm(W, NU * ROWS),
    ]
    sems = [sem((1,)) for _ in range(4)]
    sems += [sem((NU,)) for _ in range(4)]
    sems += [sem((NZ,)), sem((NZ,)), sem((NZ,)), sem((NZ - 1,))]
    sems += [sem((NU,)) for _ in range(5)]
    sems += [sem((NU, 2)), sem((NU,)), sem((NU,)), sem((7,))]
    flops = 2 * NU * ROWS * W * FF * 8
    shapes = ((T, W), (W, FF), (W, FF), (FF, W))
    results = pl.pallas_call(
        kernel,
        out_shape=tuple(pltpu.VMEM(shape, BF16) for shape in shapes),
        in_specs=[pl.BlockSpec(memory_space=pltpu.HBM)] * 7,
        out_specs=(vmem, vmem, vmem, vmem),
        scratch_shapes=scratch + sems,
        compiler_params=pltpu.CompilerParams(
            collective_id=0, has_side_effects=True, vmem_limit_bytes=50 * 1024 * 1024
        ),
        cost_estimate=pl.CostEstimate(flops=flops, bytes_accessed=12_000_000, transcendentals=0),
    )(tokens, cotangent, hbm_of(routes.T), hbm_of(gate_values.T), w_gate[0], w_up[0], w_down[0])
    token_grad, gate_grad, up_grad, down_grad = pl.pallas_call(
        write_out,
        out_shape=tuple(jax.ShapeDtypeStruct(shape, BF16) for shape in shapes),
        in_specs=[hbm] * 4,
        out_specs=(hbm,) * 4,
        scratch_shapes=[sem((sum(rows // T for rows, _ in shapes),))],
        compiler_params=pltpu.CompilerParams(vmem_limit_bytes=1024 * 1024),
    )(*(pltpu.with_memory_space_constraint(r, pltpu.VMEM) for r in results))
    return (token_grad, gate_grad[None], up_grad[None], down_grad[None])


def solution(mesh):
    return jax.shard_map(
        on_device,
        mesh=mesh,
        in_specs=(
            P("tok", "exp"),
            P("tok", "exp"),
            P("tok", None),
            P("tok", None),
            P("tok", "exp", None),
            P("tok", "exp", None),
            P("tok", None, "exp"),
        ),
        out_specs=(
            P("tok", "exp"),
            P("tok", "exp", None),
            P("tok", "exp", None),
            P("tok", None, "exp"),
        ),
        check_vma=False,
    )
```

```python
import jax
import jax.numpy as jnp
from jax import lax
from jax.experimental import pallas as pl
from jax.experimental.pallas import tpu as pltpu
from jax.sharding import PartitionSpec as P

MESH = pl.DeviceIdType.MESH
F32, BF16 = jnp.float32, jnp.bfloat16

NY, NZ, NX, NC = 4, 8, 4, 2
T = 128
CAP = 40
W = 640
FF = 1024
SH = FF // (NX * NC)
ORDER = (0, 1, 2, -2, -3, 4, 3, -1)
PART = {off: u for u, off in enumerate(ORDER)}
YOFF = (0, 1, -1, 2)
YINV = (0, 2, 1, 3)
NU = len(ORDER)
ROWS = NY * CAP
HALF = ROWS // 2
PAD = 48
DEPTH = 6


def dot(a, b):
    return jnp.dot(a, b, preferred_element_type=F32)


def dot_nt(a, b):
    return lax.dot_general(a, b, (((1,), (1,)), ((), ())), preferred_element_type=F32)


def dot_tn(a, b):
    return lax.dot_general(a, b, (((0,), (0,)), ((), ())), preferred_element_type=F32)


def kernel(
    tok_hbm, cot_hbm, ids_hbm, vals_hbm, wg_hbm, wu_hbm, wd_hbm,
    tg_ref, gg, ug, dg,
    wg, wu, wd, ids, vals, infob, zx, zd, pt, grow,
    ys, xsr, xr, sr, hp, cr, t1, t2, gb, rs, rr, zs, zr, own, xt,
    info_s, zx_s, zd_s, zr_s, ys_s, rs_s, xa_s, xb_s,
    info_r, zx_r, zd_r, zr_r, ys_r, rs_r, c1_r, t1_r, t2_r, ag_r, af_r, cg_r, in_sem,
):
    tok = lax.axis_index("tok")
    exp = lax.axis_index("exp")
    y, z = tok // NZ, lax.rem(tok, NZ)
    x, core = exp // NC, lax.rem(exp, NC)

    def at_z(off):
        return (y * NZ + lax.rem(z + off + NZ, NZ), exp)

    def at_y(off):
        return (lax.rem(y + off + NY, NY) * NZ + z, exp)

    def col(off):
        return lax.rem(x + off + NX, NX)

    def at_x(off):
        return (tok, col(off) * NC + core)

    sibling = (tok, x * NC + (1 - core))

    def rc(src, dst, s, r, dev):
        return pltpu.make_async_remote_copy(
            src_ref=src, dst_ref=dst, send_sem=s, recv_sem=r, device_id=dev, device_id_type=MESH
        )

    def bytes_of(ref, sem):
        pltpu.make_async_copy(ref, ref, sem).wait()

    def ring_copy(buf, ss, rs_, off):
        step = 1 if off > 0 else -1
        k = off % NZ
        return rc(buf.at[(off - step) % NZ], buf.at[k], ss.at[0], rs_.at[k], at_z(-step))

    def info_copy(off):
        return ring_copy(infob, info_s, info_r, off)

    def zx_copy(off):
        return ring_copy(zx, zx_s, zx_r, off)

    def zd_copy(off):
        return ring_copy(zd, zd_s, zd_r, off)

    def zr_copy(off):
        k = off % NZ - 1
        return rc(zs.at[k], zr.at[k], zr_s.at[0], zr_r.at[k], at_z(1 if off == 4 else off))

    def ys_copy(u, k):
        return rc(ys.at[u, k - 1], xsr.at[u, YINV[k]], ys_s.at[0], ys_r.at[u], at_y(YOFF[k]))

    def rs_copy(u, k):
        return rc(rs.at[u, k - 1], rr.at[u, YINV[k]], rs_s.at[0], rs_r.at[u], at_y(YOFF[k]))

    def c1_copy(u):
        return rc(hp.at[u, 1 - core], cr.at[u], xa_s.at[0], c1_r.at[u], sibling)

    def x1_copy(u, n):
        src, dst, r, to = (
            (hp.at[u, core, col(2), 0], t1.at[u, 0], t1_r, 1),
            (hp.at[u, core, col(2), 1], t1.at[u, 1], t1_r, -1),
            (hp.at[u, core, col(1), 1], t2.at[u, 0, 1], t2_r, 1),
            (hp.at[u, core, col(-1), 0], t2.at[u, 1, 0], t2_r, -1),
            (hp.at[u, core, col(1), 0], t2.at[u, 0, 0], t2_r, 1),
            (hp.at[u, core, col(-1), 1], t2.at[u, 1, 1], t2_r, -1),
        )[n]
        return rc(src, dst, xb_s.at[0], r.at[u], at_x(to))

    def ag_send(u, n):
        part, r, to = (
            (gb.at[u, core, x], ag_r.at[u, 0], 1),
            (gb.at[u, core, x], ag_r.at[u, 1], -1),
            (gb.at[u, core, col(-1), 0], af_r.at[u], 1),
            (gb.at[u, core, col(1), 1], af_r.at[u], -1),
        )[n]
        return rc(part, part, xb_s.at[0], r, at_x(to))

    def cg_send(u, off):
        part = gb.at[u, core, col(off)]
        return rc(part, part, xa_s.at[0], cg_r.at[u], sibling)

    inputs = [
        pltpu.make_async_copy(src, dst, in_sem.at[n])
        for n, (src, dst) in enumerate(
            (
                (ids_hbm, ids),
                (vals_hbm, vals),
                (tok_hbm, zx.at[0]),
                (cot_hbm, zd.at[0]),
                (wg_hbm, wg),
                (wu_hbm, wu),
                (wd_hbm, wd),
            )
        )
    ]

    def make_tables(u):
        before = (
            lax.broadcasted_iota(jnp.int32, (T, T), 0) < lax.broadcasted_iota(jnp.int32, (T, T), 1)
        ).astype(BF16)
        block = infob[ORDER[u] % NZ]
        named, value = block[0:8], block[8:16]
        masks, gates = [], []
        for k in range(NY):
            expert = (lax.rem(y + YOFF[k] + NY, NY) * NZ + z).astype(F32)
            hit = named == expert
            masks.append(jnp.sum(jnp.where(hit, 1.0, 0.0), axis=0, keepdims=True))
            gates.append(jnp.sum(jnp.where(hit, value, 0.0), axis=0, keepdims=True))
        mask_all = jnp.concatenate(masks + [jnp.zeros((8 - NY, T), F32)], axis=0)
        rank_all = dot(mask_all.astype(BF16), before)
        want = lax.broadcasted_iota(jnp.int32, (CAP, T), 0).astype(F32)
        tables, gcols = [], []
        for k in range(NY):
            on = (rank_all[k : k + 1] == want) & (mask_all[k : k + 1] > 0.5)
            tables.append(jnp.where(on, 1.0, 0.0))
            gcols.append(jnp.sum(jnp.where(on, gates[k], 0.0), axis=1, keepdims=True))
        pt[u] = jnp.concatenate(tables, axis=0).astype(BF16)
        grow[u] = jnp.concatenate(gcols, axis=0)

    def enter():
        barrier = pltpu.get_barrier_semaphore()
        partners = [at_z(off) for off in (1, -1, 2, -2, 3, -3)]
        partners += [at_y(off) for off in (1, -1, 2)] + [at_x(1), at_x(-1), sibling]
        for dev in partners:
            pl.semaphore_signal(barrier, inc=1, device_id=dev, device_id_type=MESH)
        for copy in inputs:
            copy.start()
        for copy in inputs[:4]:
            copy.wait()
        nought = jnp.zeros((2, T), F32)
        infob[0] = jnp.concatenate([ids[...].astype(F32), nought - 1.0, vals[...], nought], axis=0)
        make_tables(0)
        gather(0)
        pl.semaphore_wait(barrier, len(partners))

    def gather(u):
        k = ORDER[u] % NZ
        xs = dot(pt[u], zx[k])
        ss = dot(pt[u], zd[k]) * grow[u]
        for k in range(NY):
            both = jnp.concatenate([xs[k * CAP : (k + 1) * CAP], ss[k * CAP : (k + 1) * CAP]], axis=0)
            if k == 0:
                xsr[u, 0] = both.astype(BF16)
            else:
                ys[u, k - 1] = both.astype(BF16)

    def send_rows(u):
        for k in (3, 1, 2):
            ys_copy(u, k).start()

    def place(u):
        make_tables(u)
        gather(u)
        send_rows(u)

    def pass_x(d):
        for off in (d, -d):
            info_copy(off).wait_recv()
            zx_copy(off).wait_recv()
            if d < 3 or off > 0:
                after = off + (1 if off > 0 else -1)
                info_copy(after).start()
                zx_copy(after).start()

    def pass_d(d):
        for off in (d, -d):
            zd_copy(off).wait_recv()
            if d < 3 or off < 0:
                zd_copy(off + (1 if off > 0 else -1)).start()

    def partial(u, a, value):
        value = value.astype(BF16)
        for s in range(NX * NC):
            hp[u, s % NC, s // NC, :, a] = value[:, s * SH : (s + 1) * SH].reshape(2, HALF, SH)

    def s0(u):
        bytes_of(xsr.at[u, 1:NY], ys_r.at[u])
        both = [xsr[u, j].astype(F32) for j in range(NY)]
        rows = jnp.concatenate([v[:CAP] for v in both], axis=0).astype(BF16)
        scaled = jnp.concatenate([v[CAP:] for v in both], axis=0).astype(BF16)
        xr[u] = rows
        sr[u] = scaled
        partial(u, 0, dot(rows, wg[...]))
        partial(u, 1, dot(rows, wu[...]))
        partial(u, 2, dot_nt(scaled, wd[...]))
        c1_copy(u).start()

    def s1(u):
        c1_copy(u).wait_recv()
        for off in (2, 1, -1, 0):
            xx = col(off)
            hp[u, core, xx] = (hp[u, core, xx].astype(F32) + cr[u, xx].astype(F32)).astype(BF16)
            for n in {2: (0, 1), 1: (2,), -1: (3,), 0: ()}[off]:
                x1_copy(u, n).start()

    def s2(u):
        bytes_of(t1.at[u], t1_r.at[u])
        for n, (off, half) in enumerate(((1, 0), (-1, 1))):
            xx = col(off)
            hp[u, core, xx, half] = (hp[u, core, xx, half].astype(F32) + t1[u, n].astype(F32)).astype(BF16)
            x1_copy(u, 4 + n).start()

    def s3(u):
        bytes_of(t2.at[u], t2_r.at[u])
        for half in range(2):
            h = hp[u, core, x, half].astype(F32) + t2[u, 0, half].astype(F32) + t2[u, 1, half].astype(F32)
            h_gate, h_up, d_act = h[0], h[1], h[2]
            sigma = 1.0 / (1.0 + jnp.exp(-h_gate))
            gb[u, core, x, half, 0] = (h_gate * sigma * h_up).astype(BF16)
            gb[u, core, x, half, 1] = (d_act * h_up * sigma * (1.0 + h_gate * (1.0 - sigma))).astype(BF16)
            gb[u, core, x, half, 2] = (d_act * h_gate * sigma).astype(BF16)
        ag_send(u, 0).start()
        ag_send(u, 1).start()
        cg_send(u, 0).start()

    def s4(u):
        bytes_of(gb.at[u, core, col(-1)], ag_r.at[u, 0])
        ag_send(u, 2).start()
        bytes_of(gb.at[u, core, col(1)], ag_r.at[u, 1])
        ag_send(u, 3).start()
        cg_send(u, -1).start()
        cg_send(u, 1).start()

    def s5(u):
        bytes_of(gb.at[u, core, col(2)], af_r.at[u])
        cg_send(u, 2).start()

    def hidden(u, a):
        return jnp.concatenate(
            [gb[u, s % NC, s // NC, :, a].reshape(ROWS, SH) for s in range(NX * NC)], axis=1
        )

    def s6(u):
        bytes_of(gb.at[u, 1 - core], cg_r.at[u])
        value = dot_nt(hidden(u, 1), wg[...]) + dot_nt(hidden(u, 2), wu[...])
        nought = jnp.zeros((PAD - CAP, W), F32)
        for k in (3, 1, 2, 0):
            slot = jnp.concatenate([value[k * CAP : (k + 1) * CAP], nought], axis=0).astype(BF16)
            if k == 0:
                rr[u, 0] = slot
            else:
                rs[u, k - 1] = slot
                rs_copy(u, k).start()

    def sent_z():
        bytes_of(infob.at[0 : NZ - 1], info_s.at[0])
        bytes_of(zx.at[0 : NZ - 1], zx_s.at[0])
        bytes_of(zd.at[0 : NZ - 1], zd_s.at[0])

    def s7(u):
        bytes_of(rr.at[u, 1:NY], rs_r.at[u])
        rows = jnp.concatenate([rr[u, j].astype(F32)[:CAP] for j in range(NY)], axis=0).astype(BF16)
        value = dot_tn(pt[u], rows)
        if ORDER[u] == 0:
            own[...] = value
        else:
            zs[ORDER[u] % NZ - 1] = value.astype(BF16)
            if ORDER[u] != 3:
                zr_copy(ORDER[u]).start()

    def join():
        zr_copy(4).wait_recv()
        zs[2] = (zs[2].astype(F32) + zr[3].astype(F32)).astype(BF16)
        zr_copy(3).start()

    def step(s, carry):
        def each(stage, lag, first=0):
            @pl.when((s >= lag + first) & (s < NU + lag))
            def _():
                stage(s - lag)

        each(s1, 1)
        each(s5, 4)
        each(s4, 3, 1)
        each(s3, 2, 1)

        @pl.when(s == 3)
        def _():
            place(4)

        each(s0, 0)
        each(s2, 1)
        each(s6, 4)
        for u in range(4):

            @pl.when(s == u + 5)
            def _(u=u):
                s7(u)

        for u in range(5, NU):

            @pl.when(s == u - 2)
            def _(u=u):
                if ORDER[u] == 4:
                    info_copy(4).wait_recv()
                    zx_copy(4).wait_recv()
                    zd_copy(-4).wait_recv()
                place(u)

        return carry

    enter()
    send_rows(0)
    for off in (1, -1):
        info_copy(off).start()
    for off in (1, -1):
        zx_copy(off).start()
    for off in (1, -1):
        zd_copy(off).start()
    for copy in inputs[4:]:
        copy.wait()
    s0(0)
    pass_x(1)
    pass_d(1)
    place(1)
    s1(0)
    s2(0)
    pass_x(2)
    pass_d(2)
    place(2)
    s3(0)
    s0(1)
    s1(1)
    s4(0)
    place(3)
    s2(1)
    pass_x(3)
    pass_d(3)
    s0(2)
    lax.fori_loop(3, NU + 1, step, 0)
    s5(5)
    s4(6)
    s3(7)
    s6(5)
    s7(4)
    s5(6)
    s4(7)
    s6(6)
    s7(5)
    s5(7)
    s6(7)
    sent_z()
    s7(6)
    join()

    everything = xr[...].reshape(NU * ROWS, W)
    for n in range(W // 128):
        xt[n * 128 : (n + 1) * 128] = everything[:, n * 128 : (n + 1) * 128].T

    def all_rows(xx, a):
        return jnp.concatenate(
            [gb[:, cc, xx, :, a].reshape(NU * ROWS, SH) for cc in range(NC)], axis=1
        )

    def gate_step(xx, carry):
        at = pl.ds(pl.multiple_of(xx * 2 * SH, 2 * SH), 2 * SH)
        gg[:, at] = dot(xt[...], all_rows(xx, 1)).astype(BF16)
        return carry

    lax.fori_loop(0, NX, gate_step, 0)
    s7(7)

    def up_step(xx, carry):
        at = pl.ds(pl.multiple_of(xx * 2 * SH, 2 * SH), 2 * SH)
        ug[:, at] = dot(xt[...], all_rows(xx, 2)).astype(BF16)
        return carry

    lax.fori_loop(0, NX, up_step, 0)

    def down_step(xx, carry):
        at = pl.ds(pl.multiple_of(xx * 2 * SH, 2 * SH), 2 * SH)
        dg[at, :] = dot_tn(all_rows(xx, 0), sr[...].reshape(NU * ROWS, W)).astype(BF16)
        return carry

    lax.fori_loop(0, NX, down_step, 0)

    def finish():
        total = own[...]
        for off in (1, 2, -3, 3, -2, -1):
            zr_copy(off).wait_recv()
            total = total + zr[off % NZ - 1].astype(F32)
        tg_ref[...] = total.astype(BF16)
        bytes_of(zs, zr_s.at[0])
        bytes_of(hp, xa_s.at[0])
        bytes_of(hp.at[:, :, 0:3], xb_s.at[0])
        bytes_of(ys, ys_s.at[0])
        bytes_of(rs, rs_s.at[0])

    finish()


def write_out(*refs):
    srcs, dsts, done = refs[:4], refs[4:8], refs[8]
    copies = []
    for src, dst in zip(srcs, dsts):
        for rows in range(0, src.shape[0], T):
            part = pl.ds(rows, T)
            copies.append(pltpu.make_async_copy(src.at[part], dst.at[part], done.at[len(copies)]))
    for copy in copies:
        copy.start()
    for copy in copies:
        copy.wait()


def hbm_of(array):
    return pltpu.with_memory_space_constraint(array, pltpu.HBM)


def on_device(tokens, cotangent, routes, gate_values, w_gate, w_up, w_down):
    sem = pltpu.SemaphoreType.DMA

    def vm(*shape, dtype=BF16):
        return pltpu.VMEM(shape, dtype)

    vmem = pl.BlockSpec(memory_space=pltpu.VMEM)
    hbm = pl.BlockSpec(memory_space=pl.ANY)
    scratch = [
        vm(W, FF), vm(W, FF), vm(FF, W),
        vm(6, T, dtype=jnp.int32), vm(6, T, dtype=F32), vm(NZ, 16, T, dtype=F32),
        vm(NZ, T, W), vm(NZ, T, W),
        vm(NU, ROWS, T), vm(NU, ROWS, 1, dtype=F32),
        vm(NU, 3, 2 * CAP, W), vm(NU, NY, 2 * CAP, W),
        vm(NU, ROWS, W), vm(NU, ROWS, W),
        vm(NU, NC, NX, 2, 3, HALF, SH), vm(NU, NX, 2, 3, HALF, SH),
        vm(NU, 2, 3, HALF, SH), vm(NU, 2, 2, 3, HALF, SH),
        vm(NU, NC, NX, 2, 3, HALF, SH),
        vm(NU, 3, PAD, W), vm(NU, NY, PAD, W),
        vm(NZ - 1, T, W), vm(NZ - 1, T, W), vm(T, W, dtype=F32),
        vm(W, NU * ROWS),
    ]
    sems = [sem((1,)) for _ in range(8)]
    sems += [sem((NZ,)), sem((NZ,)), sem((NZ,)), sem((NZ - 1,))]
    sems += [sem((NU,)) for _ in range(5)]
    sems += [sem((NU, 2)), sem((NU,)), sem((NU,)), sem((7,))]
    flops = 2 * NU * ROWS * W * FF * 8
    shapes = ((T, W), (W, FF), (W, FF), (FF, W))
    results = pl.pallas_call(
        kernel,
        out_shape=tuple(pltpu.VMEM(shape, BF16) for shape in shapes),
        in_specs=[pl.BlockSpec(memory_space=pltpu.HBM)] * 7,
        out_specs=(vmem, vmem, vmem, vmem),
        scratch_shapes=scratch + sems,
        compiler_params=pltpu.CompilerParams(
            collective_id=0, has_side_effects=True, vmem_limit_bytes=50 * 1024 * 1024
        ),
        cost_estimate=pl.CostEstimate(flops=flops, bytes_accessed=12_000_000, transcendentals=0),
    )(tokens, cotangent, hbm_of(routes.T), hbm_of(gate_values.T), w_gate[0], w_up[0], w_down[0])
    token_grad, gate_grad, up_grad, down_grad = pl.pallas_call(
        write_out,
        out_shape=tuple(jax.ShapeDtypeStruct(shape, BF16) for shape in shapes),
        in_specs=[hbm] * 4,
        out_specs=(hbm,) * 4,
        scratch_shapes=[sem((sum(rows // T for rows, _ in shapes),))],
        compiler_params=pltpu.CompilerParams(vmem_limit_bytes=1024 * 1024),
    )(*(pltpu.with_memory_space_constraint(r, pltpu.VMEM) for r in results))
    return (token_grad, gate_grad[None], up_grad[None], down_grad[None])


def solution(mesh):
    return jax.shard_map(
        on_device,
        mesh=mesh,
        in_specs=(
            P("tok", "exp"),
            P("tok", "exp"),
            P("tok", None),
            P("tok", None),
            P("tok", "exp", None),
            P("tok", "exp", None),
            P("tok", None, "exp"),
        ),
        out_specs=(
            P("tok", "exp"),
            P("tok", "exp", None),
            P("tok", "exp", None),
            P("tok", None, "exp"),
        ),
        check_vma=False,
    )
```

```python
import jax
import jax.numpy as jnp
from jax import lax
from jax.experimental import pallas as pl
from jax.experimental.pallas import tpu as pltpu
from jax.sharding import PartitionSpec as P

MESH = pl.DeviceIdType.MESH
F32, BF16 = jnp.float32, jnp.bfloat16

NY, NZ, NX, NC = 4, 8, 4, 2
T = 128
CAP = 40
W = 640
FF = 1024
SH = FF // (NX * NC)
ORDER = (0, 1, 2, -2, -3, 4, 3, -1)
PART = {off: u for u, off in enumerate(ORDER)}
YOFF = (0, 1, -1, 2)
YINV = (0, 2, 1, 3)
NU = len(ORDER)
ROWS = NY * CAP
HALF = ROWS // 2
PAD = 48
DEPTH = 6


def dot(a, b):
    return jnp.dot(a, b, preferred_element_type=F32)


def dot_nt(a, b):
    return lax.dot_general(a, b, (((1,), (1,)), ((), ())), preferred_element_type=F32)


def dot_tn(a, b):
    return lax.dot_general(a, b, (((0,), (0,)), ((), ())), preferred_element_type=F32)


def kernel(
    tok_hbm, cot_hbm, ids_hbm, vals_hbm, wg_hbm, wu_hbm, wd_hbm,
    tg_ref, gg, ug, dg,
    wg, wu, wd, ids, vals, infob, zx, zd, pt, grow,
    ys, xsr, xr, sr, hp, cr, t1, t2, gb, rs, rr, zs, zr, own, xt,
    info_s, zx_s, zd_s, zr_s, ys_s, rs_s, xa_s, xb_s,
    info_r, zx_r, zd_r, zr_r, ys_r, rs_r, c1_r, t1_r, t2_r, ag_r, af_r, cg_r, in_sem,
):
    tok = lax.axis_index("tok")
    exp = lax.axis_index("exp")
    y, z = tok // NZ, lax.rem(tok, NZ)
    x, core = exp // NC, lax.rem(exp, NC)

    def at_z(off):
        return (y * NZ + lax.rem(z + off + NZ, NZ), exp)

    def at_y(off):
        return (lax.rem(y + off + NY, NY) * NZ + z, exp)

    def col(off):
        return lax.rem(x + off + NX, NX)

    def at_x(off):
        return (tok, col(off) * NC + core)

    sibling = (tok, x * NC + (1 - core))

    def rc(src, dst, s, r, dev):
        return pltpu.make_async_remote_copy(
            src_ref=src, dst_ref=dst, send_sem=s, recv_sem=r, device_id=dev, device_id_type=MESH
        )

    def bytes_of(ref, sem):
        pltpu.make_async_copy(ref, ref, sem).wait()

    def ring_copy(buf, ss, rs_, off):
        step = 1 if off > 0 else -1
        k = off % NZ
        return rc(buf.at[(off - step) % NZ], buf.at[k], ss.at[0], rs_.at[k], at_z(-step))

    def info_copy(off):
        return ring_copy(infob, info_s, info_r, off)

    def zx_copy(off):
        return ring_copy(zx, zx_s, zx_r, off)

    def zd_copy(off):
        return ring_copy(zd, zd_s, zd_r, off)

    def zr_copy(off):
        k = off % NZ - 1
        return rc(zs.at[k], zr.at[k], zr_s.at[0], zr_r.at[k], at_z(1 if off == 4 else off))

    def ys_copy(u, k):
        return rc(ys.at[u, k - 1], xsr.at[u, YINV[k]], ys_s.at[0], ys_r.at[u], at_y(YOFF[k]))

    def rs_copy(u, k):
        return rc(rs.at[u, k - 1], rr.at[u, YINV[k]], rs_s.at[0], rs_r.at[u], at_y(YOFF[k]))

    def c1_copy(u):
        return rc(hp.at[u, 1 - core], cr.at[u], xa_s.at[0], c1_r.at[u], sibling)

    def x1_copy(u, n):
        src, dst, r, to = (
            (hp.at[u, core, col(2), 0], t1.at[u, 0], t1_r, 1),
            (hp.at[u, core, col(2), 1], t1.at[u, 1], t1_r, -1),
            (hp.at[u, core, col(1), 1], t2.at[u, 0, 1], t2_r, 1),
            (hp.at[u, core, col(-1), 0], t2.at[u, 1, 0], t2_r, -1),
            (hp.at[u, core, col(1), 0], t2.at[u, 0, 0], t2_r, 1),
            (hp.at[u, core, col(-1), 1], t2.at[u, 1, 1], t2_r, -1),
        )[n]
        return rc(src, dst, xb_s.at[0], r.at[u], at_x(to))

    def ag_send(u, n):
        part, r, to = (
            (gb.at[u, core, x], ag_r.at[u, 0], 1),
            (gb.at[u, core, x], ag_r.at[u, 1], -1),
            (gb.at[u, core, col(-1), 0], af_r.at[u], 1),
            (gb.at[u, core, col(1), 1], af_r.at[u], -1),
        )[n]
        return rc(part, part, xb_s.at[0], r, at_x(to))

    def cg_send(u, off):
        part = gb.at[u, core, col(off)]
        return rc(part, part, xa_s.at[0], cg_r.at[u], sibling)

    inputs = [
        pltpu.make_async_copy(src, dst, in_sem.at[n])
        for n, (src, dst) in enumerate(
            (
                (ids_hbm, ids),
                (vals_hbm, vals),
                (tok_hbm, zx.at[0]),
                (cot_hbm, zd.at[0]),
                (wg_hbm, wg),
                (wu_hbm, wu),
                (wd_hbm, wd),
            )
        )
    ]

    def make_tables(u):
        before = (
            lax.broadcasted_iota(jnp.int32, (T, T), 0) < lax.broadcasted_iota(jnp.int32, (T, T), 1)
        ).astype(BF16)
        block = infob[ORDER[u] % NZ]
        named, value = block[0:8], block[8:16]
        masks, gates = [], []
        for k in range(NY):
            expert = (lax.rem(y + YOFF[k] + NY, NY) * NZ + z).astype(F32)
            hit = named == expert
            masks.append(jnp.sum(jnp.where(hit, 1.0, 0.0), axis=0, keepdims=True))
            gates.append(jnp.sum(jnp.where(hit, value, 0.0), axis=0, keepdims=True))
        mask_all = jnp.concatenate(masks + [jnp.zeros((8 - NY, T), F32)], axis=0)
        rank_all = dot(mask_all.astype(BF16), before)
        want = lax.broadcasted_iota(jnp.int32, (CAP, T), 0).astype(F32)
        tables, gcols = [], []
        for k in range(NY):
            on = (rank_all[k : k + 1] == want) & (mask_all[k : k + 1] > 0.5)
            tables.append(jnp.where(on, 1.0, 0.0))
            gcols.append(jnp.sum(jnp.where(on, gates[k], 0.0), axis=1, keepdims=True))
        pt[u] = jnp.concatenate(tables, axis=0).astype(BF16)
        grow[u] = jnp.concatenate(gcols, axis=0)

    def enter():
        barrier = pltpu.get_barrier_semaphore()
        partners = [at_z(off) for off in (1, -1, 2, -2, 3, -3)]
        partners += [at_y(off) for off in (1, -1, 2)] + [at_x(1), at_x(-1), sibling]
        for dev in partners:
            pl.semaphore_signal(barrier, inc=1, device_id=dev, device_id_type=MESH)
        for copy in inputs:
            copy.start()
        for copy in inputs[:4]:
            copy.wait()
        nought = jnp.zeros((2, T), F32)
        infob[0] = jnp.concatenate([ids[...].astype(F32), nought - 1.0, vals[...], nought], axis=0)
        make_tables(0)
        gather(0)
        pl.semaphore_wait(barrier, len(partners))

    def gather(u):
        k = ORDER[u] % NZ
        xs = dot(pt[u], zx[k])
        ss = dot(pt[u], zd[k]) * grow[u]
        for k in range(NY):
            both = jnp.concatenate([xs[k * CAP : (k + 1) * CAP], ss[k * CAP : (k + 1) * CAP]], axis=0)
            if k == 0:
                xsr[u, 0] = both.astype(BF16)
            else:
                ys[u, k - 1] = both.astype(BF16)

    def send_rows(u):
        for k in (3, 1, 2):
            ys_copy(u, k).start()

    def place(u):
        make_tables(u)
        gather(u)
        send_rows(u)

    def pass_x(d):
        for off in (d, -d):
            info_copy(off).wait_recv()
            zx_copy(off).wait_recv()
            if d < 3 or off > 0:
                after = off + (1 if off > 0 else -1)
                info_copy(after).start()
                zx_copy(after).start()

    def pass_d(d):
        for off in (d, -d):
            zd_copy(off).wait_recv()
            if d < 3 or off < 0:
                zd_copy(off + (1 if off > 0 else -1)).start()

    def partial(u, a, value):
        value = value.astype(BF16)
        for s in range(NX * NC):
            hp[u, s % NC, s // NC, :, a] = value[:, s * SH : (s + 1) * SH].reshape(2, HALF, SH)

    def s0(u):
        bytes_of(xsr.at[u, 1:NY], ys_r.at[u])
        both = [xsr[u, j].astype(F32) for j in range(NY)]
        rows = jnp.concatenate([v[:CAP] for v in both], axis=0).astype(BF16)
        scaled = jnp.concatenate([v[CAP:] for v in both], axis=0).astype(BF16)
        xr[u] = rows
        sr[u] = scaled
        partial(u, 0, dot(rows, wg[...]))
        partial(u, 1, dot(rows, wu[...]))
        partial(u, 2, dot_nt(scaled, wd[...]))
        c1_copy(u).start()

    def s1(u):
        c1_copy(u).wait_recv()
        for off in (2, 1, -1, 0):
            xx = col(off)
            hp[u, core, xx] = (hp[u, core, xx].astype(F32) + cr[u, xx].astype(F32)).astype(BF16)
            for n in {2: (0, 1), 1: (2,), -1: (3,), 0: ()}[off]:
                x1_copy(u, n).start()

    def s2(u):
        bytes_of(t1.at[u], t1_r.at[u])
        for n, (off, half) in enumerate(((1, 0), (-1, 1))):
            xx = col(off)
            hp[u, core, xx, half] = (hp[u, core, xx, half].astype(F32) + t1[u, n].astype(F32)).astype(BF16)
            x1_copy(u, 4 + n).start()

    def s3(u):
        bytes_of(t2.at[u], t2_r.at[u])
        for half in range(2):
            h = hp[u, core, x, half].astype(F32) + t2[u, 0, half].astype(F32) + t2[u, 1, half].astype(F32)
            h_gate, h_up, d_act = h[0], h[1], h[2]
            sigma = 1.0 / (1.0 + jnp.exp(-h_gate))
            gb[u, core, x, half, 0] = (h_gate * sigma * h_up).astype(BF16)
            gb[u, core, x, half, 1] = (d_act * h_up * sigma * (1.0 + h_gate * (1.0 - sigma))).astype(BF16)
            gb[u, core, x, half, 2] = (d_act * h_gate * sigma).astype(BF16)
        ag_send(u, 0).start()
        ag_send(u, 1).start()
        cg_send(u, 0).start()

    def s4(u):
        bytes_of(gb.at[u, core, col(-1)], ag_r.at[u, 0])
        ag_send(u, 2).start()
        bytes_of(gb.at[u, core, col(1)], ag_r.at[u, 1])
        ag_send(u, 3).start()
        cg_send(u, -1).start()
        cg_send(u, 1).start()

    def s5(u):
        bytes_of(gb.at[u, core, col(2)], af_r.at[u])
        cg_send(u, 2).start()

    def hidden(u, a):
        return jnp.concatenate(
            [gb[u, s % NC, s // NC, :, a].reshape(ROWS, SH) for s in range(NX * NC)], axis=1
        )

    def s6(u):
        bytes_of(gb.at[u, 1 - core], cg_r.at[u])
        value = dot_nt(hidden(u, 1), wg[...]) + dot_nt(hidden(u, 2), wu[...])
        nought = jnp.zeros((PAD - CAP, W), F32)
        for k in (3, 1, 2, 0):
            slot = jnp.concatenate([value[k * CAP : (k + 1) * CAP], nought], axis=0).astype(BF16)
            if k == 0:
                rr[u, 0] = slot
            else:
                rs[u, k - 1] = slot
                rs_copy(u, k).start()

    def sent_z():
        bytes_of(infob.at[0 : NZ - 1], info_s.at[0])
        bytes_of(zx.at[0 : NZ - 1], zx_s.at[0])
        bytes_of(zd.at[0 : NZ - 1], zd_s.at[0])

    def s7(u):
        bytes_of(rr.at[u, 1:NY], rs_r.at[u])
        rows = jnp.concatenate([rr[u, j].astype(F32)[:CAP] for j in range(NY)], axis=0).astype(BF16)
        value = dot_tn(pt[u], rows)
        if ORDER[u] == 0:
            own[...] = value
        else:
            zs[ORDER[u] % NZ - 1] = value.astype(BF16)
            if ORDER[u] != 3:
                zr_copy(ORDER[u]).start()

    def join():
        zr_copy(4).wait_recv()
        zs[2] = (zs[2].astype(F32) + zr[3].astype(F32)).astype(BF16)
        zr_copy(3).start()

    def step(s, carry):
        def each(stage, lag, first=0):
            @pl.when((s >= lag + first) & (s < NU + lag))
            def _():
                stage(s - lag)

        each(s1, 1)
        each(s5, 4)
        each(s4, 3, 1)
        each(s3, 2, 1)

        @pl.when(s == 3)
        def _():
            place(4)

        each(s0, 0)
        each(s2, 1)
        each(s6, 4)
        for u in range(4):

            @pl.when(s == u + 5)
            def _(u=u):
                s7(u)

        for u in range(5, NU):

            @pl.when(s == u - 2)
            def _(u=u):
                if ORDER[u] == 4:
                    info_copy(4).wait_recv()
                    zx_copy(4).wait_recv()
                    zd_copy(-4).wait_recv()
                place(u)

        return carry

    enter()
    send_rows(0)
    for off in (1, -1):
        info_copy(off).start()
    for off in (1, -1):
        zx_copy(off).start()
    for off in (1, -1):
        zd_copy(off).start()
    for copy in inputs[4:]:
        copy.wait()
    s0(0)
    pass_x(1)
    pass_d(1)
    place(1)
    s1(0)
    s2(0)
    pass_x(2)
    pass_d(2)
    place(2)
    s3(0)
    s0(1)
    s1(1)
    s4(0)
    place(3)
    s2(1)
    pass_x(3)
    pass_d(3)
    s0(2)
    lax.fori_loop(3, NU + 1, step, 0)
    s5(5)
    s4(6)
    s3(7)
    s6(5)
    s7(4)
    s5(6)
    s4(7)
    s6(6)
    s7(5)
    s5(7)
    s6(7)
    sent_z()
    s7(6)
    join()

    everything = xr[...].reshape(NU * ROWS, W)
    for n in range(W // 128):
        xt[n * 128 : (n + 1) * 128] = everything[:, n * 128 : (n + 1) * 128].T

    def all_rows(xx, a):
        return jnp.concatenate(
            [gb[:, cc, xx, :, a].reshape(NU * ROWS, SH) for cc in range(NC)], axis=1
        )

    def gate_step(xx, carry):
        at = pl.ds(pl.multiple_of(xx * 2 * SH, 2 * SH), 2 * SH)
        gg[:, at] = dot(xt[...], all_rows(xx, 1)).astype(BF16)
        return carry

    lax.fori_loop(0, NX // 2, gate_step, 0)
    s7(7)
    lax.fori_loop(NX // 2, NX, gate_step, 0)

    def up_step(xx, carry):
        at = pl.ds(pl.multiple_of(xx * 2 * SH, 2 * SH), 2 * SH)
        ug[:, at] = dot(xt[...], all_rows(xx, 2)).astype(BF16)
        return carry

    lax.fori_loop(0, NX, up_step, 0)

    def down_step(xx, carry):
        at = pl.ds(pl.multiple_of(xx * 2 * SH, 2 * SH), 2 * SH)
        dg[at, :] = dot_tn(all_rows(xx, 0), sr[...].reshape(NU * ROWS, W)).astype(BF16)
        return carry

    lax.fori_loop(0, NX, down_step, 0)

    def finish():
        total = own[...]
        for off in (1, 2, -3, 3, -2, -1):
            zr_copy(off).wait_recv()
            total = total + zr[off % NZ - 1].astype(F32)
        tg_ref[...] = total.astype(BF16)
        bytes_of(zs, zr_s.at[0])
        bytes_of(hp, xa_s.at[0])
        bytes_of(hp.at[:, :, 0:3], xb_s.at[0])
        bytes_of(ys, ys_s.at[0])
        bytes_of(rs, rs_s.at[0])

    finish()


def write_out(*refs):
    srcs, dsts, done = refs[:4], refs[4:8], refs[8]
    copies = []
    for src, dst in zip(srcs, dsts):
        for rows in range(0, src.shape[0], T):
            part = pl.ds(rows, T)
            copies.append(pltpu.make_async_copy(src.at[part], dst.at[part], done.at[len(copies)]))
    for copy in copies:
        copy.start()
    for copy in copies:
        copy.wait()


def hbm_of(array):
    return pltpu.with_memory_space_constraint(array, pltpu.HBM)


def on_device(tokens, cotangent, routes, gate_values, w_gate, w_up, w_down):
    sem = pltpu.SemaphoreType.DMA

    def vm(*shape, dtype=BF16):
        return pltpu.VMEM(shape, dtype)

    vmem = pl.BlockSpec(memory_space=pltpu.VMEM)
    hbm = pl.BlockSpec(memory_space=pl.ANY)
    scratch = [
        vm(W, FF), vm(W, FF), vm(FF, W),
        vm(6, T, dtype=jnp.int32), vm(6, T, dtype=F32), vm(NZ, 16, T, dtype=F32),
        vm(NZ, T, W), vm(NZ, T, W),
        vm(NU, ROWS, T), vm(NU, ROWS, 1, dtype=F32),
        vm(NU, 3, 2 * CAP, W), vm(NU, NY, 2 * CAP, W),
        vm(NU, ROWS, W), vm(NU, ROWS, W),
        vm(NU, NC, NX, 2, 3, HALF, SH), vm(NU, NX, 2, 3, HALF, SH),
        vm(NU, 2, 3, HALF, SH), vm(NU, 2, 2, 3, HALF, SH),
        vm(NU, NC, NX, 2, 3, HALF, SH),
        vm(NU, 3, PAD, W), vm(NU, NY, PAD, W),
        vm(NZ - 1, T, W), vm(NZ - 1, T, W), vm(T, W, dtype=F32),
        vm(W, NU * ROWS),
    ]
    sems = [sem((1,)) for _ in range(8)]
    sems += [sem((NZ,)), sem((NZ,)), sem((NZ,)), sem((NZ - 1,))]
    sems += [sem((NU,)) for _ in range(5)]
    sems += [sem((NU, 2)), sem((NU,)), sem((NU,)), sem((7,))]
    flops = 2 * NU * ROWS * W * FF * 8
    shapes = ((T, W), (W, FF), (W, FF), (FF, W))
    results = pl.pallas_call(
        kernel,
        out_shape=tuple(pltpu.VMEM(shape, BF16) for shape in shapes),
        in_specs=[pl.BlockSpec(memory_space=pltpu.HBM)] * 7,
        out_specs=(vmem, vmem, vmem, vmem),
        scratch_shapes=scratch + sems,
        compiler_params=pltpu.CompilerParams(
            collective_id=0, has_side_effects=True, vmem_limit_bytes=50 * 1024 * 1024
        ),
        cost_estimate=pl.CostEstimate(flops=flops, bytes_accessed=12_000_000, transcendentals=0),
    )(tokens, cotangent, hbm_of(routes.T), hbm_of(gate_values.T), w_gate[0], w_up[0], w_down[0])
    token_grad, gate_grad, up_grad, down_grad = pl.pallas_call(
        write_out,
        out_shape=tuple(jax.ShapeDtypeStruct(shape, BF16) for shape in shapes),
        in_specs=[hbm] * 4,
        out_specs=(hbm,) * 4,
        scratch_shapes=[sem((sum(rows // T for rows, _ in shapes),))],
        compiler_params=pltpu.CompilerParams(vmem_limit_bytes=1024 * 1024),
    )(*(pltpu.with_memory_space_constraint(r, pltpu.VMEM) for r in results))
    return (token_grad, gate_grad[None], up_grad[None], down_grad[None])


def solution(mesh):
    return jax.shard_map(
        on_device,
        mesh=mesh,
        in_specs=(
            P("tok", "exp"),
            P("tok", "exp"),
            P("tok", None),
            P("tok", None),
            P("tok", "exp", None),
            P("tok", "exp", None),
            P("tok", None, "exp"),
        ),
        out_specs=(
            P("tok", "exp"),
            P("tok", "exp", None),
            P("tok", "exp", None),
            P("tok", None, "exp"),
        ),
        check_vma=False,
    )
```
